128 devices in a mesh: row: 32 (over z, y, core), col: 4 (over x).
Axes of the slice: x: 4, y: 4, z: 4, core: 2. Of those that a mesh axis runs over, the one named last changes fastest.
Arguments:
- source_vectors: bfloat16 [256, 512, 768], P('row'), may hold values from -5 to 5
- target_vectors: bfloat16 [64, 512, 768], P('row', 'col'), may hold values from -1 to 1
- pair_list: int32 [256, 12], P('row'), may hold values from 0 to 63, as said below
- counts: int32 [256], P('row'), may hold values from 4 to 12, as said below
- owner_map: int32 [64], replicated, may hold values from 0 to 63, as said below
Outputs:
- source_dual: float32 [256, 512], P('row')
- target_dual: float32 [64, 512], P('row', 'col')
The draws below stay inside these ranges and needn't reach their ends.
Inputs may be any that keep to these rules, and one draw needn't show every extreme that they name: `pair_list`: source blocks 4 m to 4 m + 3 list the same ids in the same order. The 12 ids of one source block differ, and so do all ids listed by the source blocks 8 r, 8 r + 4, ... up to 8 r + 4 for each r; their storage slots owner_map[id] fall at most 1 times into any range of slots 2 o to 2 o + 1, and exactly 1 times into some. Source block s uses the first counts[s] of its listed ids; both ends of the range occur. `owner_map`: A permutation of the storage slots.
All inputs are finite; a program needn't handle non-finite values.
Results may differ from the reference program's by a relative error of at most 0.0003.
Values may be sent and summed in bfloat16 or wider, within the bound.
No kernel may reach another device: no remote copies, remote signals or barrier semaphores. Data moves between devices by JAX's collectives and lax.ppermute only.
A program may use at most 128 MiB of HBM per device.

```python
import jax
import jax.numpy as jnp
from jax import lax

WIDTH = 768
BLOCK = 512
LISTED = 12
FEWEST = 4
SHARE = 4
SWEEPS = 3
SRC_BLOCKS = 8
TGT_BLOCKS = 2
SOURCES = 256
TARGETS = 64
N_ROW = 32


def block_plan(key):
    key_order, key_shift, key_place, key_count = jax.random.split(key, 4)
    groups = SRC_BLOCKS // SHARE
    orders = jax.vmap(lambda single: jax.random.permutation(single, N_ROW))(jax.random.split(key_order, N_ROW))
    entry_ids = jnp.arange(groups * LISTED, dtype=jnp.int32)
    owner_rows = orders[:, entry_ids % N_ROW].astype(jnp.int32)
    ranking = entry_ids // N_ROW
    shifts = jax.random.randint(key_shift, (N_ROW, N_ROW), 0, TGT_BLOCKS, dtype=jnp.int32)
    bases = jnp.take_along_axis(shifts, owner_rows, axis=1)
    local_index = (bases + 2 * ranking[None, :]) % TGT_BLOCKS
    grouped = (owner_rows * TGT_BLOCKS + local_index).reshape(N_ROW, groups, 1, LISTED)
    stored = jnp.broadcast_to(grouped, (N_ROW, groups, SHARE, LISTED)).reshape(SOURCES, LISTED)
    placing = jax.random.permutation(key_place, TARGETS).astype(jnp.int32)
    inverse = jnp.argsort(placing).astype(jnp.int32)
    pair_list = inverse[stored]
    counts = jax.random.randint(key_count, (SOURCES,), FEWEST, LISTED + 1, dtype=jnp.int32)
    counts = counts.at[0].set(LISTED).at[SOURCES - 1].set(FEWEST)
    return (pair_list, counts, placing)


def draw_pair_list(key, part):
    return block_plan(key)[0]


def draw_counts(key, part):
    return block_plan(key)[1]


def draw_owner_map(key, part):
    return block_plan(key)[2]


def draw_target_vectors(key, part):
    key = jax.random.fold_in(key, 7)
    values = jnp.clip(jax.random.normal(key, (TARGETS, BLOCK, WIDTH), jnp.float32) * 0.05, -0.3, 0.3)
    return values.astype(jnp.bfloat16)


def draw_source_vectors(key, part):
    key = jax.random.fold_in(key, 5)
    values = jnp.clip(jax.random.normal(key, (SOURCES, BLOCK, WIDTH), jnp.float32) * 0.05, -0.3, 0.3)
    return values.astype(jnp.bfloat16)


def setup_inputs(seed: int = 0) -> dict:
    key_list = jax.random.split(jax.random.key(seed), 6)
    return {
        "source_vectors": draw_source_vectors(jax.random.fold_in(key_list[5], 71), 0),
        "target_vectors": draw_target_vectors(jax.random.fold_in(key_list[5], 71), 0),
        "pair_list": draw_pair_list(jax.random.fold_in(key_list[5], 71), 0),
        "counts": draw_counts(jax.random.fold_in(key_list[5], 71), 0),
        "owner_map": draw_owner_map(jax.random.fold_in(key_list[5], 71), 0),
    }


EPSILON = 0.05
NEGATIVE = -1.0e30


def reference(source_vectors, target_vectors, pair_list, counts, owner_map):
    stored = owner_map[pair_list].astype(jnp.int32)
    alive_mask = jnp.arange(LISTED, dtype=jnp.int32)[None, :] < counts[:, None]
    target_dual = jnp.zeros((TARGETS, BLOCK), jnp.float32)
    source_dual = jnp.zeros((SOURCES, BLOCK), jnp.float32)
    for sweep_index in range(SWEEPS):
        def one_block(running, inputs):
            maxima, totals = running
            source_rows, slots_here, alive_here = inputs
            gathered = target_vectors[slots_here].astype(jnp.float32)
            scores = jnp.einsum("id,kjd->kij", source_rows.astype(jnp.float32), gathered)
            logits = (target_dual[slots_here][:, None, :] + scores) / EPSILON
            logits = jnp.where(alive_here[:, None, None], logits, NEGATIVE)
            row_peak = jnp.maximum(jnp.max(logits, axis=(0, 2)), 0.0)
            row_total = jnp.exp(-row_peak) + jnp.sum(jnp.exp(logits - row_peak[None, :, None]), axis=(0, 2))
            dual_rows = -EPSILON * (row_peak + jnp.log(row_total))
            columns = (dual_rows[None, :, None] + scores) / EPSILON
            column_peak = jnp.max(columns, axis=1)
            column_total = jnp.sum(jnp.exp(columns - column_peak[:, None, :]), axis=1)
            column_peak = jnp.where(alive_here[:, None], column_peak, NEGATIVE)
            column_total = jnp.where(alive_here[:, None], column_total, 0.0)
            old_peak = maxima[slots_here]
            old_total = totals[slots_here]
            new_peak = jnp.maximum(old_peak, column_peak)
            new_total = old_total * jnp.exp(old_peak - new_peak) + column_total * jnp.exp(column_peak - new_peak)
            return (maxima.at[slots_here].set(new_peak), totals.at[slots_here].set(new_total)), dual_rows

        initial = (jnp.zeros((TARGETS, BLOCK), jnp.float32), jnp.ones((TARGETS, BLOCK), jnp.float32))
        (maxima, totals), source_dual = lax.scan(one_block, initial, (source_vectors, stored, alive_mask))
        target_dual = -EPSILON * (maxima + jnp.log(totals))
    return source_dual, target_dual
```

```python
import functools

import jax
import jax.numpy as jnp
import numpy as np
from jax import lax
from jax.experimental import pallas as pl
from jax.experimental.pallas import tpu as pltpu
from jax.sharding import PartitionSpec as P

SHARE = 4
SWEEPS = 3
EPSILON = 0.05
CHUNKS = (64, 64)
LOG2E = 1.4426950408889634
LN2 = 0.6931471805599453
SCALE = LOG2E / EPSILON
NEGATIVE = -1e30
MIB = 2**20


def row_perm(dz, dy, dc):
    return [
        ((z * 4 + y) * 2 + c, (((z + dz) % 4) * 4 + (y + dy) % 4) * 2 + (c ^ dc))
        for z in range(4)
        for y in range(4)
        for c in range(2)
    ]


def send(x, dz, dy, dc):
    return lax.ppermute(x, "row", row_perm(dz, dy, dc))


RING = (0, -1, 1, 2)


def ring_gather(own, dz, dy):
    half = own.shape[1] // 2
    before = send(own, dz, dy, 0)
    after = send(own, -dz, -dy, 0)
    far_low = send(before[:, :half], dz, dy, 0)
    far_high = send(after[:, half:], -dz, -dy, 0)
    far = jnp.concatenate([far_low, far_high], axis=1)
    return jnp.concatenate([own, before, after, far], axis=0)


def ring_spread(four, dz, dy):
    before = send(four, dz, dy, 0)
    after = send(four, -dz, -dy, 0)
    far_low = send(before[:2], dz, dy, 0)
    far_high = send(after[2:], -dz, -dy, 0)
    return [four, before, after, far_low, far_high]


def gather_plane(blocks):
    first = ring_gather(blocks[:1], 0, 1)
    second = ring_gather(blocks[1:], 1, 0)
    mine = ring_spread(first, 1, 0) + ring_spread(second, 0, 1)
    return mine + [send(piece, 0, 0, 1) for piece in mine]


def piece_layout():
    entries = []
    for core in range(2):
        for which in range(2):
            for part in range(5):
                across = (0, -1, 1, 2, 2)[part]
                for index, along in enumerate((RING, RING, RING, RING[:2], RING[2:])[part]):
                    dz, dy = (across, along) if which == 0 else (along, across)
                    entries.append(((core * 2 + which) * 5 + part, index, dz, dy, core, which))
    return entries


def make_score_kernel(rows):
    def kernel(dest, counts, source, *refs):
        pieces = refs[:20]
        kernel_out, peak_out, high_out, total_out, held, sums, sems = refs[20:]
        layout = piece_layout()
        step = pl.program_id(0)
        group = step // SHARE
        listed = kernel_out.shape[1]

        def fetch(piece, index, entry):
            return pltpu.make_async_copy(
                pieces[piece].at[index], held.at[pl.ds(entry * rows, rows)], sems.at[entry]
            )

        @pl.when(step == 0)
        def _():
            for number, (piece, index, *_) in enumerate(layout):

                @pl.when(dest[number] >= 0)
                def _():
                    fetch(piece, index, dest[number]).start()

        for g in range(2):

            @pl.when(step == SHARE * g)
            def _():
                for k in range(listed):
                    fetch(0, 0, g * listed + k).wait()

        live = counts[step]

        def batch(first, size):
            base = pl.multiple_of((group * listed + first) * rows, rows)
            scores = lax.dot_general(
                held[pl.ds(base, size * rows), :],
                source[0],
                (((1,), (1,)), ((), ())),
                preferred_element_type=jnp.float32,
            )
            for p in range(size):
                one = scores[p * rows : (p + 1) * rows] * SCALE
                peak = jnp.max(one, axis=0, keepdims=True)
                raised = jnp.exp2(one - peak)
                kernel_out[0, first + p] = raised
                peak_out[0, pl.ds(first + p, 1), :] = peak
                sums[pl.ds(first + p, 1), :] = jnp.sum(raised, axis=0, keepdims=True)

        big = 512 // rows
        small = 128 // rows
        bigs = live // big
        done = bigs * big

        def big_step(q, carry):
            batch(q * big, big)
            return carry

        def small_step(q, carry):
            batch(done + q * small, small)
            return carry

        lax.fori_loop(0, bigs, big_step, 0)
        lax.fori_loop(0, (live - done + small - 1) // small, small_step, 0)
        alive = lax.broadcasted_iota(jnp.int32, sums.shape, 0) < live
        peaks = jnp.where(alive, peak_out[0], NEGATIVE)
        peak_out[0] = peaks
        high = jnp.max(peaks, axis=0, keepdims=True)
        total = jnp.sum(
            jnp.where(alive, sums[...] * jnp.exp2(peaks - high), 0.0), axis=0, keepdims=True
        )
        high_out[pl.ds(step, 1), :] = high
        total_out[pl.ds(step, 1), :] = total

    return kernel


def score_stage(rows, dest, counts, source_vectors, pieces, listed):
    blocks, block_rows, width = source_vectors.shape
    padded = 16
    return pl.pallas_call(
        make_score_kernel(rows),
        grid_spec=pltpu.PrefetchScalarGridSpec(
            num_scalar_prefetch=2,
            grid=(blocks,),
            in_specs=[pl.BlockSpec((1, block_rows, width), lambda s, *_: (s, 0, 0))]
            + [pl.BlockSpec(memory_space=pl.ANY)] * len(pieces),
            out_specs=[
                pl.BlockSpec((1, listed, rows, block_rows), lambda s, *_: (s, 0, 0, 0)),
                pl.BlockSpec((1, padded, block_rows), lambda s, *_: (s, 0, 0)),
                pl.BlockSpec((blocks, block_rows), lambda s, *_: (0, 0)),
                pl.BlockSpec((blocks, block_rows), lambda s, *_: (0, 0)),
            ],
            scratch_shapes=[
                pltpu.VMEM((2 * listed * rows, width), jnp.bfloat16),
                pltpu.VMEM((padded, block_rows), jnp.float32),
                pltpu.SemaphoreType.DMA((2 * listed,)),
            ],
        ),
        out_shape=[
            jax.ShapeDtypeStruct((blocks, listed, rows, block_rows), jnp.float32),
            jax.ShapeDtypeStruct((blocks, padded, block_rows), jnp.float32),
            jax.ShapeDtypeStruct((blocks, block_rows), jnp.float32),
            jax.ShapeDtypeStruct((blocks, block_rows), jnp.float32),
        ],
        compiler_params=pltpu.CompilerParams(vmem_limit_bytes=24 * MIB),
        cost_estimate=pl.CostEstimate(
            flops=2 * blocks * listed * rows * block_rows * width,
            bytes_accessed=4 * blocks * listed * rows * block_rows,
            transcendentals=0,
        ),
        name="scores",
    )(dest, counts, source_vectors, *pieces)


def column_kernel(chunks, final, counts, slots, level, part, near, far, back, *refs):
    n = len(chunks)
    matrices, peaks = refs[:n], refs[n : 2 * n]
    sums_out = refs[2 * n]
    weights, columns = refs[-2:]
    blocks, block_rows = part.shape
    listed = matrices[0].shape[1]
    total = part[...] + near[...] + far[...] + back[...] + jnp.exp2(-level[...])
    inverse = 1.0 / total
    if final:
        refs[2 * n + 1][...] = -EPSILON * LN2 * (level[...] + jnp.log2(total))
    for c in range(n):
        for s in range(blocks):
            weights[c, s] = jnp.exp2(peaks[c][s] - level[s : s + 1, :]) * inverse[s : s + 1, :]
    sums_out[...] = jnp.zeros_like(sums_out)
    for g in range(blocks // SHARE):
        longest = functools.reduce(jnp.maximum, [counts[g * SHARE + m] for m in range(SHARE)])

        def one_entry(k, carry):
            for c, rows in enumerate(chunks):
                start = sum(chunks[:c])
                columns[start : start + rows, :] = jnp.zeros((rows, 128), jnp.float32)
            for m in range(SHARE):
                s = g * SHARE + m

                @pl.when(k < counts[s])
                def _():
                    for c, rows in enumerate(chunks):
                        start = sum(chunks[:c])
                        w = weights[c, s, pl.ds(k, 1), :]
                        spread = [
                            jnp.broadcast_to(w[:, 128 * l : 128 * l + 128], (8, 128))
                            for l in range(block_rows // 128)
                        ]
                        for j in range(0, rows, 8):
                            piece = columns[start + j : start + j + 8, :]
                            for l, ws in enumerate(spread):
                                piece = piece + matrices[c][s, k, j : j + 8, 128 * l : 128 * l + 128] * ws
                            columns[start + j : start + j + 8, :] = piece

            row = jnp.sum(columns[...].T, axis=0, keepdims=True)
            sums_out[pl.ds(slots[g * listed + k], 1), :] = row
            return carry

        lax.fori_loop(0, longest, one_entry, 0)


def column_pass(chunks, final, counts, slots, targets, level, parts, matrices, peaks):
    blocks, block_rows = level.shape
    n = len(chunks)
    vmem = pl.BlockSpec(memory_space=pltpu.VMEM)
    smem = pl.BlockSpec(memory_space=pltpu.SMEM)
    out_shape = [jax.ShapeDtypeStruct((targets, 128), jnp.float32)]
    if final:
        out_shape.append(jax.ShapeDtypeStruct((blocks, block_rows), jnp.float32))
    return pl.pallas_call(
        functools.partial(column_kernel, chunks, final),
        in_specs=[smem, smem] + [vmem] * (5 + 2 * n),
        out_specs=[vmem] * len(out_shape),
        out_shape=out_shape,
        scratch_shapes=[
            pltpu.VMEM((n,) + peaks[0].shape, jnp.float32),
            pltpu.VMEM((sum(chunks), 128), jnp.float32),
        ],
        compiler_params=pltpu.CompilerParams(vmem_limit_bytes=8 * MIB),
        name="columns",
    )(counts, slots, level, *parts, *matrices, *peaks)


def row_kernel(chunks, counts, slots, level, sums, *refs):
    n = len(chunks)
    matrices, peaks = refs[:n], refs[n : 2 * n]
    out, weights, gathered, spread = refs[2 * n :]
    blocks, block_rows = out.shape
    listed = matrices[0].shape[1]
    for e in range(2 * listed):
        gathered[e : e + 1, :] = sums[pl.ds(slots[e], 1), :]
    factors = (1.0 / (1.0 + gathered[...])).T
    for e in range(2 * listed):
        spread[e] = jnp.broadcast_to(factors[:, e : e + 1], (128, 128))
    for c in range(n):
        for s in range(blocks):
            weights[c, s] = jnp.exp2(peaks[c][s] - level[s : s + 1, :])
    lanes = block_rows // 128
    for s in range(blocks):
        g = s // SHARE

        def one_entry(k, total):
            for c, rows in enumerate(chunks):
                start = sum(chunks[:c])
                acc = [jnp.zeros((8, 128), jnp.float32) for _ in range(lanes)]
                for j in range(0, rows, 8):
                    v = spread[g * listed + k, start + j : start + j + 8, :]
                    for l in range(lanes):
                        acc[l] = acc[l] + matrices[c][s, k, j : j + 8, 128 * l : 128 * l + 128] * v
                w = weights[c, s, pl.ds(k, 1), :]
                total = tuple(t + a * w[:, 128 * l : 128 * l + 128] for l, (t, a) in enumerate(zip(total, acc)))
            return total

        total = lax.fori_loop(
            0, counts[s], one_entry, tuple(jnp.zeros((8, 128), jnp.float32) for _ in range(lanes))
        )
        out[s : s + 1, :] = jnp.concatenate([jnp.sum(t, axis=0, keepdims=True) for t in total], axis=1)


def row_pass(chunks, counts, slots, level, sums, matrices, peaks):
    blocks, block_rows = level.shape
    listed = matrices[0].shape[1]
    n = len(chunks)
    vmem = pl.BlockSpec(memory_space=pltpu.VMEM)
    smem = pl.BlockSpec(memory_space=pltpu.SMEM)
    return pl.pallas_call(
        functools.partial(row_kernel, chunks),
        in_specs=[smem, smem] + [vmem] * (2 + 2 * n),
        out_specs=vmem,
        out_shape=jax.ShapeDtypeStruct((blocks, block_rows), jnp.float32),
        scratch_shapes=[
            pltpu.VMEM((n,) + peaks[0].shape, jnp.float32),
            pltpu.VMEM((128, 128), jnp.float32),
            pltpu.VMEM((2 * listed, 128, 128), jnp.float32),
        ],
        compiler_params=pltpu.CompilerParams(vmem_limit_bytes=8 * MIB),
        name="rows",
    )(counts, slots, level, sums, *matrices, *peaks)


def from_columns(x):
    return [x] + [lax.ppermute(x, "col", [(i, (i + d) % 4) for i in range(4)]) for d in (1, 2, 3)]


def sum_over_rows(x):
    x = x + send(x, 0, 0, 1)
    x = x + send(x, 0, 1, 0) + send(x, 0, 2, 0) + send(x, 0, 3, 0)
    return x + send(x, 1, 0, 0) + send(x, 2, 0, 0) + send(x, 3, 0, 0)


def shards(source_vectors, target_vectors, pair_list, counts, owner_map):
    blocks = source_vectors.shape[0]
    target_blocks, quarter, _ = target_vectors.shape
    listed = pair_list.shape[1]
    targets = owner_map.shape[0]
    lead = pair_list.reshape(blocks // SHARE, SHARE, listed)[:, 0, :].reshape(-1)
    lookup = lead[:, None] == jnp.arange(targets, dtype=jnp.int32)[None, :]
    slots = jnp.sum(jnp.where(lookup, owner_map[None, :], 0), axis=1)
    me = lax.axis_index("row")
    z, y, core = me // 8, (me // 2) % 4, me % 2
    layout = np.array(piece_layout(), np.int32)
    owner = (((z + layout[:, 2]) % 4) * 4 + (y + layout[:, 3]) % 4) * 2 + (core ^ layout[:, 4])
    held_slot = owner * target_blocks + layout[:, 5]
    entry_ids = jnp.arange(2 * listed, dtype=jnp.int32)
    dest = jnp.max(jnp.where(held_slot[:, None] == slots[None, :], entry_ids[None, :], -1), axis=1)

    matrices, peaks, highs, totals = [], [], [], []
    start = 0
    for rows in CHUNKS:
        pieces = gather_plane(target_vectors[:, start : start + rows])
        start += rows
        matrix, peak, high, total = score_stage(rows, dest, counts, source_vectors, pieces, listed)
        matrices.append(matrix)
        peaks.append(peak)
        highs.append(high)
        totals.append(total)
    high = functools.reduce(jnp.maximum, highs)
    total = sum(t * jnp.exp2(h - high) for t, h in zip(totals, highs))
    both = from_columns(jnp.stack([high, total]))
    level = jnp.maximum(functools.reduce(jnp.maximum, [b[0] for b in both]), 0.0)
    parts = [b[1] * jnp.exp2(b[0] - level) for b in both]

    for sweep_index in range(SWEEPS):
        final = sweep_index == SWEEPS - 1
        sums = column_pass(
            CHUNKS, final, counts, slots, targets, level, parts, matrices, peaks
        )
        if final:
            break
        sums = sum_over_rows(sums[0])
        parts = from_columns(row_pass(CHUNKS, counts, slots, level, sums, matrices, peaks))
    sums, source_dual = sums
    row_count = targets // target_blocks
    back = lax.all_to_all(
        sums.reshape(row_count, target_blocks, quarter), "row", split_axis=0, concat_axis=0, tiled=True
    )
    target_dual = -EPSILON * jnp.log(1.0 + jnp.sum(back, axis=0))
    return source_dual, target_dual


def solution(mesh):
    return jax.shard_map(
        shards,
        mesh=mesh,
        in_specs=(P("row", None, None), P("row", "col", None), P("row", None), P("row"), P()),
        out_specs=(P("row", None), P("row", "col")),
        check_vma=False,
    )
```

```python
import functools

import jax
import jax.numpy as jnp
import numpy as np
from jax import lax
from jax.experimental import pallas as pl
from jax.experimental.pallas import tpu as pltpu
from jax.sharding import PartitionSpec as P

SHARE = 4
SWEEPS = 3
EPSILON = 0.05
LOG2E = 1.4426950408889634
LN2 = 0.6931471805599453
SCALE = LOG2E / EPSILON
NEGATIVE = -1e30
MIB = 2**20


def row_perm(dz, dy, dc):
    return [
        ((z * 4 + y) * 2 + c, (((z + dz) % 4) * 4 + (y + dy) % 4) * 2 + (c ^ dc))
        for z in range(4)
        for y in range(4)
        for c in range(2)
    ]


def send(x, dz, dy, dc):
    return lax.ppermute(x, "row", row_perm(dz, dy, dc))


RING = (0, -1, 1, 2)
STAGES = 3


def tie(*arrays):
    return lax.optimization_barrier(arrays)


def ring_gather(own, dz, dy):
    parts = [own, send(own, dz, dy, 0), send(own, -dz, -dy, 0), send(own, 2 * dz, 2 * dy, 0)]
    return jnp.concatenate(parts, axis=0)


def piece_layout():
    first = [(core, which, 0, RING) for core in range(2) for which in range(2)]
    second = [(core, which, d, RING) for core in range(2) for which in range(2) for d in (-1, 1)]
    third = [
        (core, which, 2, half) for core in range(2) for which in range(2) for half in (RING[:2], RING[2:])
    ]
    stages = []
    for pieces in (first, second, third):
        entries = []
        for piece, (core, which, across, ring) in enumerate(pieces):
            for index, along in enumerate(ring):
                dz, dy = (across, along) if which == 0 else (along, across)
                entries.append((piece, index, dz, dy, core, which))
        stages.append(entries)
    return stages


def score_kernel(stage, listed, dest, segments, lives, source, *refs):
    layout = piece_layout()[stage]
    number = max(entry[0] for entry in layout) + 1
    pieces, refs = refs[:number], refs[number:]
    if stage > 0:
        (_, peak_in, sum_in), refs = refs[:3], refs[3:]
    matrix, peak_out, sum_out = refs[:3]
    if stage == STAGES - 1:
        high_out, total_out = refs[3:5]
    held, raised, tally, fetch_sems, store_sems = refs[-5:]
    step = pl.program_id(0)
    group = step // SHARE
    rows = held.shape[0] // (2 * listed + 4)
    buffers = raised.shape[0]

    def fetch(piece, index, entry):
        return pltpu.make_async_copy(
            pieces[piece].at[index], held.at[pl.ds(entry * rows, rows)], fetch_sems.at[entry]
        )

    def store(buffer, entry):
        return pltpu.make_async_copy(raised.at[buffer], matrix.at[step, entry], store_sems.at[buffer])

    @pl.when(step == 0)
    def _():
        tally[0] = 0
        for position, (piece, index, *_) in enumerate(layout):

            @pl.when(dest[position] >= 0)
            def _():
                fetch(piece, index, dest[position]).start()

    for g in range(2):

        @pl.when(step == SHARE * g)
        def _():
            def arrive(entry, carry):
                fetch(0, 0, g * listed + entry).wait()
                return carry

            lax.fori_loop(segments[g * (STAGES + 1) + stage], segments[g * (STAGES + 1) + stage + 1], arrive, 0)

    if stage > 0:
        peak_out[...] = peak_in[...]
        sum_out[...] = sum_in[...]
    else:
        peak_out[...] = jnp.full(peak_out.shape, NEGATIVE, jnp.float32)
        sum_out[...] = jnp.zeros(sum_out.shape, jnp.float32)
    begin = segments[group * (STAGES + 1) + stage]
    live = lives[step * STAGES + stage]

    def batch(first, size, spare):
        base = pl.multiple_of((group * listed + begin + first) * rows, rows)
        scores = lax.dot_general(
            held[pl.ds(base, size * rows), :],
            source[0],
            (((1,), (1,)), ((), ())),
            preferred_element_type=jnp.float32,
        )

        def finish(p):
            count = tally[0] + first + p
            buffer = lax.rem(count, buffers)

            @pl.when(count >= buffers)
            def _():
                store(buffer, 0).wait()

            one = scores[p * rows : (p + 1) * rows] * SCALE
            peak = jnp.max(one, axis=0, keepdims=True)
            lifted = jnp.exp2(one - peak)
            raised[buffer] = lifted
            peak_out[0, pl.ds(begin + first + p, 1), :] = peak
            sum_out[0, pl.ds(begin + first + p, 1), :] = jnp.sum(lifted, axis=0, keepdims=True)
            store(buffer, begin + first + p).start()

        for p in range(size):
            if p < size - spare:
                finish(p)
            else:
                pl.when(first + p < live)(functools.partial(finish, p))

    def four(q, carry):
        batch(4 * q, 4, 0)
        return carry

    def two(q, carry):
        batch(4 * (live // 4) + 2 * q, 2, 1)
        return carry

    lax.fori_loop(0, live // 4, four, 0)
    lax.fori_loop(0, (live % 4 + 1) // 2, two, 0)
    tally[0] = tally[0] + live

    @pl.when(step == pl.num_programs(0) - 1)
    def _():
        for buffer in range(buffers):

            @pl.when(tally[0] > buffer)
            def _():
                store(buffer, 0).wait()

    if stage == STAGES - 1:
        high = jnp.max(peak_out[0], axis=0, keepdims=True)
        high_out[pl.ds(step, 1), :] = high
        total_out[pl.ds(step, 1), :] = jnp.sum(
            sum_out[0] * jnp.exp2(peak_out[0] - high), axis=0, keepdims=True
        )


def score_stage(stage, listed, dest, segments, lives, source_vectors, pieces, earlier):
    blocks, block_rows, width = source_vectors.shape
    rows = pieces[0].shape[1]
    padded = 16
    hbm = pl.BlockSpec(memory_space=pltpu.HBM)
    small = pl.BlockSpec((1, padded, block_rows), lambda s, *_: (s, 0, 0))
    whole = pl.BlockSpec((blocks, block_rows), lambda s, *_: (0, 0))
    last = stage == STAGES - 1
    share = (0.25, 0.5, 0.25)[stage]
    return pl.pallas_call(
        functools.partial(score_kernel, stage, listed),
        grid_spec=pltpu.PrefetchScalarGridSpec(
            num_scalar_prefetch=3,
            grid=(blocks,),
            in_specs=[pl.BlockSpec((1, block_rows, width), lambda s, *_: (s, 0, 0))]
            + [hbm] * len(pieces)
            + [hbm, small, small][: len(earlier)],
            out_specs=[hbm, small, small] + [whole, whole] * last,
            scratch_shapes=[
                pltpu.VMEM(((2 * listed + 4) * rows, width), jnp.bfloat16),
                pltpu.VMEM((8, rows, block_rows), jnp.float32),
                pltpu.SMEM((1,), jnp.int32),
                pltpu.SemaphoreType.DMA((2 * listed,)),
                pltpu.SemaphoreType.DMA((8,)),
            ],
        ),
        out_shape=[
            jax.ShapeDtypeStruct((blocks, listed, rows, block_rows), jnp.float32),
            jax.ShapeDtypeStruct((blocks, padded, block_rows), jnp.float32),
            jax.ShapeDtypeStruct((blocks, padded, block_rows), jnp.float32),
        ]
        + [jax.ShapeDtypeStruct((blocks, block_rows), jnp.float32)] * 2 * last,
        input_output_aliases={4 + len(pieces): 0} if earlier else {},
        compiler_params=pltpu.CompilerParams(vmem_limit_bytes=24 * MIB),
        cost_estimate=pl.CostEstimate(
            flops=int(2 * blocks * listed * rows * block_rows * width * share),
            bytes_accessed=int(4 * blocks * listed * rows * block_rows * share),
            transcendentals=0,
        ),
        name="scores",
    )(dest, segments, lives, source_vectors, *pieces, *earlier)


def column_kernel(final, counts, slots, order, level, part, near, far, back, matrix, peaks, *refs):
    sums_out = refs[0]
    weights, columns = refs[-2:]
    blocks, block_rows = part.shape
    listed, rows = matrix.shape[1:3]
    total = part[...] + near[...] + far[...] + back[...] + jnp.exp2(-level[...])
    inverse = 1.0 / total
    if final:
        refs[1][...] = -EPSILON * LN2 * (level[...] + jnp.log2(total))
    for s in range(blocks):
        weights[s] = jnp.exp2(peaks[s] - level[s : s + 1, :]) * inverse[s : s + 1, :]
    sums_out[...] = jnp.zeros_like(sums_out)
    for g in range(blocks // SHARE):

        def one_entry(k, carry):
            columns[...] = jnp.zeros_like(columns)
            for m in range(SHARE):
                s = g * SHARE + m

                @pl.when(order[(blocks + s) * listed + k] > 0)
                def _():
                    w = weights[s, pl.ds(k, 1), :]
                    spread = [
                        jnp.broadcast_to(w[:, 128 * l : 128 * l + 128], (8, 128))
                        for l in range(block_rows // 128)
                    ]
                    for j in range(0, rows, 8):
                        piece = columns[j : j + 8, :]
                        for l, ws in enumerate(spread):
                            piece = piece + matrix[s, k, j : j + 8, 128 * l : 128 * l + 128] * ws
                        columns[j : j + 8, :] = piece

            row = jnp.sum(columns[...].T, axis=0, keepdims=True)
            sums_out[pl.ds(slots[g * listed + k], 1), :] = row
            return carry

        lax.fori_loop(0, listed, one_entry, 0)


def column_pass(final, counts, slots, order, targets, level, parts, matrix, peaks):
    blocks, block_rows = level.shape
    rows = matrix.shape[2]
    vmem = pl.BlockSpec(memory_space=pltpu.VMEM)
    smem = pl.BlockSpec(memory_space=pltpu.SMEM)
    out_shape = [jax.ShapeDtypeStruct((targets, rows), jnp.float32)]
    if final:
        out_shape.append(jax.ShapeDtypeStruct((blocks, block_rows), jnp.float32))
    return pl.pallas_call(
        functools.partial(column_kernel, final),
        in_specs=[smem] * 3 + [vmem] * 7,
        out_specs=[vmem] * len(out_shape),
        out_shape=out_shape,
        scratch_shapes=[
            pltpu.VMEM(peaks.shape, jnp.float32),
            pltpu.VMEM((rows, 128), jnp.float32),
        ],
        compiler_params=pltpu.CompilerParams(vmem_limit_bytes=8 * MIB),
        name="columns",
    )(counts, slots, order, level, *parts, matrix, peaks)


def row_kernel(counts, slots, order, level, sums, matrix, peaks, out, weights, gathered, spread):
    blocks, block_rows = out.shape
    listed, rows = matrix.shape[1:3]
    for e in range(2 * listed):
        gathered[e : e + 1, :] = sums[pl.ds(slots[e], 1), :]
    factors = (1.0 / (1.0 + gathered[...])).T
    for e in range(2 * listed):
        spread[e] = jnp.broadcast_to(factors[:, e : e + 1], (rows, 128))
    for s in range(blocks):
        weights[s] = jnp.exp2(peaks[s] - level[s : s + 1, :])
    lanes = block_rows // 128
    for s in range(blocks):
        g = s // SHARE

        def one_entry(t, total):
            k = order[s * listed + t]
            acc = [jnp.zeros((8, 128), jnp.float32) for _ in range(lanes)]
            for j in range(0, rows, 8):
                v = spread[g * listed + k, j : j + 8, :]
                for l in range(lanes):
                    acc[l] = acc[l] + matrix[s, k, j : j + 8, 128 * l : 128 * l + 128] * v
            w = weights[s, pl.ds(k, 1), :]
            return tuple(t + a * w[:, 128 * l : 128 * l + 128] for l, (t, a) in enumerate(zip(total, acc)))

        total = lax.fori_loop(
            0, counts[s], one_entry, tuple(jnp.zeros((8, 128), jnp.float32) for _ in range(lanes))
        )
        out[s : s + 1, :] = jnp.concatenate([jnp.sum(t, axis=0, keepdims=True) for t in total], axis=1)


def row_pass(counts, slots, order, level, sums, matrix, peaks):
    blocks, block_rows = level.shape
    listed, rows = matrix.shape[1:3]
    vmem = pl.BlockSpec(memory_space=pltpu.VMEM)
    smem = pl.BlockSpec(memory_space=pltpu.SMEM)
    return pl.pallas_call(
        row_kernel,
        in_specs=[smem] * 3 + [vmem] * 4,
        out_specs=vmem,
        out_shape=jax.ShapeDtypeStruct((blocks, block_rows), jnp.float32),
        scratch_shapes=[
            pltpu.VMEM(peaks.shape, jnp.float32),
            pltpu.VMEM((128, rows), jnp.float32),
            pltpu.VMEM((2 * listed, rows, 128), jnp.float32),
        ],
        compiler_params=pltpu.CompilerParams(vmem_limit_bytes=8 * MIB),
        name="rows",
    )(counts, slots, order, level, sums, matrix, peaks)


def from_columns(x):
    return [x] + [lax.ppermute(x, "col", [(i, (i + d) % 4) for i in range(4)]) for d in (1, 2, 3)]


def sum_over_rows(x):
    x = x + send(x, 0, 0, 1)
    x = x + send(x, 0, 1, 0) + send(x, 0, 2, 0) + send(x, 0, 3, 0)
    return x + send(x, 1, 0, 0) + send(x, 2, 0, 0) + send(x, 3, 0, 0)


def tables(pair_list, counts, owner_map, target_blocks):
    blocks, listed = pair_list.shape
    groups = blocks // SHARE
    targets = owner_map.shape[0]
    lead = pair_list.reshape(groups, SHARE, listed)[:, 0, :]
    lookup = lead[:, :, None] == jnp.arange(targets, dtype=jnp.int32)
    stored = jnp.sum(jnp.where(lookup, owner_map, 0), axis=2)
    me = lax.axis_index("row")
    z, y, core = me // 8, (me // 2) % 4, me % 2
    stages = piece_layout()
    layout = np.array([entry for stage in stages for entry in stage], np.int32)
    stage_at = np.array([n for n, stage in enumerate(stages) for _ in stage], np.int32)
    owner = (((z + layout[:, 2]) % 4) * 4 + (y + layout[:, 3]) % 4) * 2 + (core ^ layout[:, 4])
    held_slot = owner * target_blocks + layout[:, 5]
    match = held_slot[:, None, None] == stored[None]
    stage_of = jnp.sum(jnp.where(match, stage_at[:, None, None], 0), axis=0)
    ids = jnp.arange(listed, dtype=jnp.int32)
    rank = stage_of * listed + ids
    place = jnp.sum((rank[:, None, :] < rank[:, :, None]).astype(jnp.int32), axis=2)
    offset = jnp.arange(groups, dtype=jnp.int32)[:, None] * listed
    dest = jnp.sum(jnp.where(match, offset + place + 1, 0), axis=(1, 2)) - 1
    bounds = jnp.arange(STAGES + 1, dtype=jnp.int32)
    segments = jnp.sum((stage_of[:, None, :] < bounds[:, None]).astype(jnp.int32), axis=2)
    alive = ids[None, :] < counts[:, None]
    stage_rows = jnp.repeat(stage_of, SHARE, axis=0)
    lives = jnp.sum((alive[:, None, :] & (stage_rows[:, None, :] == bounds[:STAGES, None])).astype(jnp.int32), axis=2)
    at_place = place[:, None, :] == ids[None, :, None]
    slots = jnp.sum(jnp.where(at_place, stored[:, None, :], 0), axis=2)
    alive_at = jnp.any(jnp.repeat(at_place, SHARE, axis=0) & alive[:, None, :], axis=2)
    turn = jnp.sum((alive_at[:, None, :] & (ids[None, :] < ids[:, None])[None]).astype(jnp.int32), axis=2)
    order = jnp.sum(
        jnp.where(alive_at[:, None, :] & (turn[:, None, :] == ids[None, :, None]), ids[None, None, :], 0), axis=2
    )
    order = jnp.concatenate([order.reshape(-1), alive_at.astype(jnp.int32).reshape(-1)])
    cuts = np.cumsum([len(stage) for stage in stages])[:-1]
    return slots.reshape(-1), jnp.split(dest, cuts), segments.reshape(-1), lives.reshape(-1), order


def shards(source_vectors, target_vectors, pair_list, counts, owner_map):
    target_blocks, quarter, _ = target_vectors.shape
    listed = pair_list.shape[1]
    targets = owner_map.shape[0]
    slots, dest, segments, lives, order = tables(pair_list, counts, owner_map, target_blocks)

    def across(pieces):
        return pieces + [send(piece, 0, 0, 1) for piece in pieces]

    def stage(number, pieces, earlier):
        return score_stage(
            number, listed, dest[number], segments, lives, source_vectors, across(pieces), earlier
        )

    first = [ring_gather(target_vectors[:1], 0, 1), ring_gather(target_vectors[1:], 1, 0)]
    second = [
        send(first[0], 1, 0, 0),
        send(first[0], -1, 0, 0),
        send(first[1], 0, 1, 0),
        send(first[1], 0, -1, 0),
    ]
    done = stage(0, first, [])
    *second, peaks = tie(*second, done[1])
    third = [
        send(second[0][:2], 1, 0, 0),
        send(second[1][2:], -1, 0, 0),
        send(second[2][:2], 0, 1, 0),
        send(second[3][2:], 0, -1, 0),
    ]
    done = stage(1, second, [done[0], peaks, done[2]])
    *third, peaks = tie(*third, done[1])
    matrix, peaks, _, high, total = stage(2, third, [done[0], peaks, done[2]])

    both = from_columns(jnp.stack([high, total]))
    level = jnp.maximum(functools.reduce(jnp.maximum, [b[0] for b in both]), 0.0)
    parts = [b[1] * jnp.exp2(b[0] - level) for b in both]

    for sweep_index in range(SWEEPS):
        final = sweep_index == SWEEPS - 1
        sums = column_pass(final, counts, slots, order, targets, level, parts, matrix, peaks)
        if final:
            break
        sums = sum_over_rows(sums[0])
        parts = from_columns(row_pass(counts, slots, order, level, sums, matrix, peaks))
    sums, source_dual = sums
    row_count = targets // target_blocks
    back = lax.all_to_all(
        sums.reshape(row_count, target_blocks, quarter), "row", split_axis=0, concat_axis=0, tiled=True
    )
    target_dual = -EPSILON * jnp.log(1.0 + jnp.sum(back, axis=0))
    return source_dual, target_dual


def solution(mesh):
    return jax.shard_map(
        shards,
        mesh=mesh,
        in_specs=(P("row", None, None), P("row", "col", None), P("row", None), P("row"), P()),
        out_specs=(P("row", None), P("row", "col")),
        check_vma=False,
    )
```

```python
import functools

import jax
import jax.numpy as jnp
import numpy as np
from jax import lax
from jax.experimental import pallas as pl
from jax.experimental.pallas import tpu as pltpu
from jax.sharding import PartitionSpec as P

SHARE = 4
SWEEPS = 3
EPSILON = 0.05
LOG2E = 1.4426950408889634
LN2 = 0.6931471805599453
SCALE = LOG2E / EPSILON
NEGATIVE = -1e30
MIB = 2**20


def row_perm(dz, dy, dc):
    return [
        ((z * 4 + y) * 2 + c, (((z + dz) % 4) * 4 + (y + dy) % 4) * 2 + (c ^ dc))
        for z in range(4)
        for y in range(4)
        for c in range(2)
    ]


def send(x, dz, dy, dc):
    return lax.ppermute(x, "row", row_perm(dz, dy, dc))


RING = (0, -1, 1, 2)
STAGES = 3


def tie(*arrays):
    return lax.optimization_barrier(arrays)


def ring_gather(own, dz, dy):
    parts = [own, send(own, dz, dy, 0), send(own, -dz, -dy, 0), send(own, 2 * dz, 2 * dy, 0)]
    return jnp.concatenate(parts, axis=0)


def piece_layout():
    first = [(core, which, 0, RING) for core in range(2) for which in range(2)]
    second = [(core, which, d, RING) for core in range(2) for which in range(2) for d in (-1, 1)]
    third = [
        (core, which, 2, half) for core in range(2) for which in range(2) for half in (RING[:2], RING[2:])
    ]
    stages = []
    for pieces in (first, second, third):
        entries = []
        for piece, (core, which, across, ring) in enumerate(pieces):
            for index, along in enumerate(ring):
                dz, dy = (across, along) if which == 0 else (along, across)
                entries.append((piece, index, dz, dy, core, which))
        stages.append(entries)
    return stages


def score_kernel(stage, listed, dest, segments, lives, source, *refs):
    layout = piece_layout()[stage]
    number = max(entry[0] for entry in layout) + 1
    pieces, refs = refs[:number], refs[number:]
    if stage > 0:
        refs = refs[3:]
    matrix, peak_out, sum_out = refs[:3]
    if stage == STAGES - 1:
        high_out, total_out = refs[3:5]
    held, streamed, fetch_sems, stream_sems = refs[-4:]
    blocks = source.shape[0]
    rows = matrix.shape[2]

    def stream(s):
        return pltpu.make_async_copy(source.at[s], streamed.at[lax.rem(s, 2)], stream_sems.at[lax.rem(s, 2)])

    stream(0).start()

    def fetch(piece, index, entry):
        return pltpu.make_async_copy(
            pieces[piece].at[index], held.at[pl.ds(entry * rows, rows)], fetch_sems.at[entry]
        )

    for position, (piece, index, *_) in enumerate(layout):

        @pl.when(dest[position] >= 0)
        def _():
            fetch(piece, index, dest[position]).start()

    if stage == 0:
        peak_out[...] = jnp.full(peak_out.shape, NEGATIVE, jnp.float32)
        sum_out[...] = jnp.zeros(sum_out.shape, jnp.float32)

    def one_block(s, carry):
        group = s // SHARE
        begin = segments[group * (STAGES + 1) + stage]
        live = lives[s * STAGES + stage]

        @pl.when(lax.rem(s, SHARE) == 0)
        def _():
            def arrive(entry, carry):
                fetch(0, 0, group * listed + entry).wait()
                return carry

            lax.fori_loop(begin, segments[group * (STAGES + 1) + stage + 1], arrive, 0)

        @pl.when(s + 1 < blocks)
        def _():
            stream(s + 1).start()

        stream(s).wait()

        def batch(first, size):
            base = pl.multiple_of((group * listed + begin + first) * rows, rows)
            scores = lax.dot_general(
                held[pl.ds(base, size * rows), :],
                streamed[lax.rem(s, 2)],
                (((1,), (1,)), ((), ())),
                preferred_element_type=jnp.float32,
            )
            for p in range(size):
                one = scores[p * rows : (p + 1) * rows] * SCALE
                peak = jnp.max(one, axis=0, keepdims=True)
                lifted = jnp.exp2(one - peak)
                matrix[s, begin + first + p] = lifted
                peak_out[s, pl.ds(begin + first + p, 1), :] = peak
                sum_out[s, pl.ds(begin + first + p, 1), :] = jnp.sum(lifted, axis=0, keepdims=True)

        def four(q, carry):
            batch(4 * q, 4)
            return carry

        lax.fori_loop(0, live // 4, four, 0)
        for size in (1, 2, 3):
            pl.when(lax.rem(live, 4) == size)(functools.partial(batch, live - size, size))
        return carry

    lax.fori_loop(0, blocks, one_block, 0)
    if stage == STAGES - 1:
        for s in range(blocks):
            high = jnp.max(peak_out[s], axis=0, keepdims=True)
            high_out[s : s + 1, :] = high
            total_out[s : s + 1, :] = jnp.sum(sum_out[s] * jnp.exp2(peak_out[s] - high), axis=0, keepdims=True)


def score_stage(stage, listed, dest, segments, lives, source_vectors, pieces, earlier):
    blocks, block_rows, width = source_vectors.shape
    rows = pieces[0].shape[1]
    padded = 16
    hbm = pl.BlockSpec(memory_space=pltpu.HBM)
    vmem = pl.BlockSpec(memory_space=pltpu.VMEM)
    smem = pl.BlockSpec(memory_space=pltpu.SMEM)
    last = stage == STAGES - 1
    share = (0.25, 0.5, 0.25)[stage]
    small = jax.ShapeDtypeStruct((blocks, padded, block_rows), jnp.float32)
    whole = jax.ShapeDtypeStruct((blocks, block_rows), jnp.float32)
    if earlier:
        earlier = [pltpu.with_memory_space_constraint(earlier[0], pltpu.VMEM)] + earlier[1:]
    return pl.pallas_call(
        functools.partial(score_kernel, stage, listed),
        in_specs=[smem] * 3 + [hbm] * (1 + len(pieces)) + [vmem] * len(earlier),
        out_specs=[vmem] * (3 + 2 * last),
        out_shape=[pltpu.VMEM((blocks, listed, rows, block_rows), jnp.float32), small, small] + [whole] * 2 * last,
        scratch_shapes=[
            pltpu.VMEM((2 * listed * rows, width), jnp.bfloat16),
            pltpu.VMEM((2, block_rows, width), jnp.bfloat16),
            pltpu.SemaphoreType.DMA((2 * listed,)),
            pltpu.SemaphoreType.DMA((2,)),
        ],
        input_output_aliases={4 + len(pieces) + n: n for n in range(len(earlier))},
        compiler_params=pltpu.CompilerParams(vmem_limit_bytes=12 * MIB),
        cost_estimate=pl.CostEstimate(
            flops=int(2 * blocks * listed * rows * block_rows * width * share),
            bytes_accessed=int(4 * blocks * listed * rows * block_rows * share),
            transcendentals=0,
        ),
        name="scores",
    )(dest, segments, lives, source_vectors, *pieces, *earlier)


def column_kernel(final, counts, slots, order, level, part, near, far, back, matrix, peaks, *refs):
    sums_out = refs[0]
    weights, columns = refs[-2:]
    blocks, block_rows = part.shape
    listed, rows = matrix.shape[1:3]
    total = part[...] + near[...] + far[...] + back[...] + jnp.exp2(-level[...])
    inverse = 1.0 / total
    if final:
        refs[1][...] = -EPSILON * LN2 * (level[...] + jnp.log2(total))
    for s in range(blocks):
        weights[s] = jnp.exp2(peaks[s] - level[s : s + 1, :]) * inverse[s : s + 1, :]
    sums_out[...] = jnp.zeros_like(sums_out)
    for g in range(blocks // SHARE):

        def one_entry(k, carry):
            columns[...] = jnp.zeros_like(columns)
            for m in range(SHARE):
                s = g * SHARE + m

                @pl.when(order[(blocks + s) * listed + k] > 0)
                def _():
                    w = weights[s, pl.ds(k, 1), :]
                    spread = [
                        jnp.broadcast_to(w[:, 128 * l : 128 * l + 128], (8, 128))
                        for l in range(block_rows // 128)
                    ]
                    for j in range(0, rows, 8):
                        piece = columns[j : j + 8, :]
                        for l, ws in enumerate(spread):
                            piece = piece + matrix[s, k, j : j + 8, 128 * l : 128 * l + 128] * ws
                        columns[j : j + 8, :] = piece

            row = jnp.sum(columns[...].T, axis=0, keepdims=True)
            sums_out[pl.ds(slots[g * listed + k], 1), :] = row
            return carry

        lax.fori_loop(0, listed, one_entry, 0)


def column_pass(final, counts, slots, order, targets, level, parts, matrix, peaks):
    blocks, block_rows = level.shape
    rows = matrix.shape[2]
    vmem = pl.BlockSpec(memory_space=pltpu.VMEM)
    smem = pl.BlockSpec(memory_space=pltpu.SMEM)
    out_shape = [jax.ShapeDtypeStruct((targets, rows), jnp.float32)]
    if final:
        out_shape.append(jax.ShapeDtypeStruct((blocks, block_rows), jnp.float32))
    return pl.pallas_call(
        functools.partial(column_kernel, final),
        in_specs=[smem] * 3 + [vmem] * 7,
        out_specs=[vmem] * len(out_shape),
        out_shape=out_shape,
        scratch_shapes=[
            pltpu.VMEM(peaks.shape, jnp.float32),
            pltpu.VMEM((rows, 128), jnp.float32),
        ],
        compiler_params=pltpu.CompilerParams(vmem_limit_bytes=8 * MIB),
        name="columns",
    )(counts, slots, order, level, *parts, matrix, peaks)


def row_kernel(counts, slots, order, level, sums, matrix, peaks, out, weights, gathered, spread):
    blocks, block_rows = out.shape
    listed, rows = matrix.shape[1:3]
    for e in range(2 * listed):
        gathered[e : e + 1, :] = sums[pl.ds(slots[e], 1), :]
    factors = (1.0 / (1.0 + gathered[...])).T
    for e in range(2 * listed):
        spread[e] = jnp.broadcast_to(factors[:, e : e + 1], (rows, 128))
    for s in range(blocks):
        weights[s] = jnp.exp2(peaks[s] - level[s : s + 1, :])
    lanes = block_rows // 128
    for s in range(blocks):
        g = s // SHARE

        def one_entry(t, total):
            k = order[s * listed + t]
            acc = [jnp.zeros((8, 128), jnp.float32) for _ in range(lanes)]
            for j in range(0, rows, 8):
                v = spread[g * listed + k, j : j + 8, :]
                for l in range(lanes):
                    acc[l] = acc[l] + matrix[s, k, j : j + 8, 128 * l : 128 * l + 128] * v
            w = weights[s, pl.ds(k, 1), :]
            return tuple(t + a * w[:, 128 * l : 128 * l + 128] for l, (t, a) in enumerate(zip(total, acc)))

        total = lax.fori_loop(
            0, counts[s], one_entry, tuple(jnp.zeros((8, 128), jnp.float32) for _ in range(lanes))
        )
        out[s : s + 1, :] = jnp.concatenate([jnp.sum(t, axis=0, keepdims=True) for t in total], axis=1)


def row_pass(counts, slots, order, level, sums, matrix, peaks):
    blocks, block_rows = level.shape
    listed, rows = matrix.shape[1:3]
    vmem = pl.BlockSpec(memory_space=pltpu.VMEM)
    smem = pl.BlockSpec(memory_space=pltpu.SMEM)
    return pl.pallas_call(
        row_kernel,
        in_specs=[smem] * 3 + [vmem] * 4,
        out_specs=vmem,
        out_shape=jax.ShapeDtypeStruct((blocks, block_rows), jnp.float32),
        scratch_shapes=[
            pltpu.VMEM(peaks.shape, jnp.float32),
            pltpu.VMEM((128, rows), jnp.float32),
            pltpu.VMEM((2 * listed, rows, 128), jnp.float32),
        ],
        compiler_params=pltpu.CompilerParams(vmem_limit_bytes=8 * MIB),
        name="rows",
    )(counts, slots, order, level, sums, matrix, peaks)


def from_columns(x):
    return [x] + [lax.ppermute(x, "col", [(i, (i + d) % 4) for i in range(4)]) for d in (1, 2, 3)]


def sum_over_rows(x):
    x = x + send(x, 0, 0, 1)
    x = x + send(x, 0, 1, 0) + send(x, 0, 2, 0) + send(x, 0, 3, 0)
    return x + send(x, 1, 0, 0) + send(x, 2, 0, 0) + send(x, 3, 0, 0)


def tables(pair_list, counts, owner_map, target_blocks):
    blocks, listed = pair_list.shape
    groups = blocks // SHARE
    targets = owner_map.shape[0]
    lead = pair_list.reshape(groups, SHARE, listed)[:, 0, :]
    lookup = lead[:, :, None] == jnp.arange(targets, dtype=jnp.int32)
    stored = jnp.sum(jnp.where(lookup, owner_map, 0), axis=2)
    me = lax.axis_index("row")
    z, y, core = me // 8, (me // 2) % 4, me % 2
    stages = piece_layout()
    layout = np.array([entry for stage in stages for entry in stage], np.int32)
    stage_at = np.array([n for n, stage in enumerate(stages) for _ in stage], np.int32)
    owner = (((z + layout[:, 2]) % 4) * 4 + (y + layout[:, 3]) % 4) * 2 + (core ^ layout[:, 4])
    held_slot = owner * target_blocks + layout[:, 5]
    match = held_slot[:, None, None] == stored[None]
    stage_of = jnp.sum(jnp.where(match, stage_at[:, None, None], 0), axis=0)
    ids = jnp.arange(listed, dtype=jnp.int32)
    rank = stage_of * listed + ids
    place = jnp.sum((rank[:, None, :] < rank[:, :, None]).astype(jnp.int32), axis=2)
    offset = jnp.arange(groups, dtype=jnp.int32)[:, None] * listed
    dest = jnp.sum(jnp.where(match, offset + place + 1, 0), axis=(1, 2)) - 1
    bounds = jnp.arange(STAGES + 1, dtype=jnp.int32)
    segments = jnp.sum((stage_of[:, None, :] < bounds[:, None]).astype(jnp.int32), axis=2)
    alive = ids[None, :] < counts[:, None]
    stage_rows = jnp.repeat(stage_of, SHARE, axis=0)
    lives = jnp.sum((alive[:, None, :] & (stage_rows[:, None, :] == bounds[:STAGES, None])).astype(jnp.int32), axis=2)
    at_place = place[:, None, :] == ids[None, :, None]
    slots = jnp.sum(jnp.where(at_place, stored[:, None, :], 0), axis=2)
    alive_at = jnp.any(jnp.repeat(at_place, SHARE, axis=0) & alive[:, None, :], axis=2)
    turn = jnp.sum((alive_at[:, None, :] & (ids[None, :] < ids[:, None])[None]).astype(jnp.int32), axis=2)
    order = jnp.sum(
        jnp.where(alive_at[:, None, :] & (turn[:, None, :] == ids[None, :, None]), ids[None, None, :], 0), axis=2
    )
    order = jnp.concatenate([order.reshape(-1), alive_at.astype(jnp.int32).reshape(-1)])
    cuts = np.cumsum([len(stage) for stage in stages])[:-1]
    return slots.reshape(-1), jnp.split(dest, cuts), segments.reshape(-1), lives.reshape(-1), order


def shards(source_vectors, target_vectors, pair_list, counts, owner_map):
    target_blocks, quarter, _ = target_vectors.shape
    listed = pair_list.shape[1]
    targets = owner_map.shape[0]
    source_vectors = pltpu.with_memory_space_constraint(source_vectors, pltpu.HBM)
    slots, dest, segments, lives, order = tables(pair_list, counts, owner_map, target_blocks)

    def across(pieces):
        pieces = pieces + [send(piece, 0, 0, 1) for piece in pieces]
        return [pltpu.with_memory_space_constraint(piece, pltpu.HBM) for piece in pieces]

    def stage(number, pieces, earlier):
        return score_stage(
            number, listed, dest[number], segments, lives, source_vectors, across(pieces), earlier
        )

    first = [ring_gather(target_vectors[:1], 0, 1), ring_gather(target_vectors[1:], 1, 0)]
    *first, slots, segments, lives, order, early, later, latest = tie(*first, slots, segments, lives, order, *dest)
    dest = [early, later, latest]
    second = [
        send(first[0], 1, 0, 0),
        send(first[0], -1, 0, 0),
        send(first[1], 0, 1, 0),
        send(first[1], 0, -1, 0),
    ]
    done = stage(0, first, [])
    *second, peaks = tie(*second, done[1])
    third = [
        send(second[0][:2], 1, 0, 0),
        send(second[1][2:], -1, 0, 0),
        send(second[2][:2], 0, 1, 0),
        send(second[3][2:], 0, -1, 0),
    ]
    done = stage(1, second, [done[0], peaks, done[2]])
    *third, peaks = tie(*third, done[1])
    matrix, peaks, _, high, total = stage(2, third, [done[0], peaks, done[2]])
    matrix = pltpu.with_memory_space_constraint(matrix, pltpu.VMEM)

    both = from_columns(jnp.stack([high, total]))
    level = jnp.maximum(functools.reduce(jnp.maximum, [b[0] for b in both]), 0.0)
    parts = [b[1] * jnp.exp2(b[0] - level) for b in both]

    for sweep_index in range(SWEEPS):
        final = sweep_index == SWEEPS - 1
        sums = column_pass(final, counts, slots, order, targets, level, parts, matrix, peaks)
        if final:
            break
        sums = sum_over_rows(sums[0])
        parts = from_columns(row_pass(counts, slots, order, level, sums, matrix, peaks))
    sums, source_dual = sums
    row_count = targets // target_blocks
    back = lax.all_to_all(
        sums.reshape(row_count, target_blocks, quarter), "row", split_axis=0, concat_axis=0, tiled=True
    )
    target_dual = -EPSILON * jnp.log(1.0 + jnp.sum(back, axis=0))
    return source_dual, target_dual


def solution(mesh):
    return jax.shard_map(
        shards,
        mesh=mesh,
        in_specs=(P("row", None, None), P("row", "col", None), P("row", None), P("row"), P()),
        out_specs=(P("row", None), P("row", "col")),
        check_vma=False,
    )
```

```python
import functools

import jax
import jax.numpy as jnp
import numpy as np
from jax import lax
from jax.experimental import pallas as pl
from jax.experimental.pallas import tpu as pltpu
from jax.sharding import PartitionSpec as P

SHARE = 4
SWEEPS = 3
EPSILON = 0.05
LOG2E = 1.4426950408889634
LN2 = 0.6931471805599453
SCALE = LOG2E / EPSILON
NEGATIVE = -1e30
MIB = 2**20


def row_perm(dz, dy, dc):
    return [
        ((z * 4 + y) * 2 + c, (((z + dz) % 4) * 4 + (y + dy) % 4) * 2 + (c ^ dc))
        for z in range(4)
        for y in range(4)
        for c in range(2)
    ]


def send(x, dz, dy, dc):
    return lax.ppermute(x, "row", row_perm(dz, dy, dc))


RING = (0, -1, 1, 2)
STAGES = 3


def tie(*arrays):
    return lax.optimization_barrier(arrays)


def ring_sends(own, dz, dy):
    return [send(own, dz, dy, 0), send(own, -dz, -dy, 0), send(own, 2 * dz, 2 * dy, 0)]


def piece_layout():
    first = [(core, which, 0, RING) for core in range(2) for which in range(2)]
    second = [(core, which, d, RING) for core in range(2) for which in range(2) for d in (-1, 1)]
    third = [
        (core, which, 2, half) for core in range(2) for which in range(2) for half in (RING[:2], RING[2:])
    ]
    stages = []
    for pieces in (first, second, third):
        entries = []
        for piece, (core, which, across, ring) in enumerate(pieces):
            for index, along in enumerate(ring):
                dz, dy = (across, along) if which == 0 else (along, across)
                entries.append((piece, index, dz, dy, core, which))
        stages.append(entries)
    return stages


def score_kernel(stage, listed, dest, segments, lives, source, *refs):
    layout = piece_layout()[stage]
    number = max(entry[0] for entry in layout) + 1
    pieces, refs = refs[:number], refs[number:]
    if stage > 0:
        refs = refs[3:]
    matrix, peak_out, sum_out = refs[:3]
    if stage == STAGES - 1:
        high_out, total_out = refs[3:5]
    held, streamed, fetch_sems, stream_sems = refs[-4:]
    blocks = source.shape[0]
    rows = matrix.shape[2]

    def stream(s):
        return pltpu.make_async_copy(source.at[s], streamed.at[lax.rem(s, 2)], stream_sems.at[lax.rem(s, 2)])

    stream(0).start()

    def fetch(piece, index, entry):
        return pltpu.make_async_copy(
            pieces[piece].at[index], held.at[pl.ds(entry * rows, rows)], fetch_sems.at[entry]
        )

    offset = sum(len(entries) for entries in piece_layout()[:stage])
    for position, (piece, index, *_) in enumerate(layout, offset):

        @pl.when(dest[position] >= 0)
        def _():
            fetch(piece, index, dest[position]).start()

    if stage == 0:
        peak_out[...] = jnp.full(peak_out.shape, NEGATIVE, jnp.float32)
        sum_out[...] = jnp.zeros(sum_out.shape, jnp.float32)

    def one_block(s, carry):
        group = s // SHARE
        begin = segments[group * (STAGES + 1) + stage]
        live = lives[s * STAGES + stage]

        @pl.when(lax.rem(s, SHARE) == 0)
        def _():
            def arrive(entry, carry):
                fetch(0, 0, group * listed + entry).wait()
                return carry

            lax.fori_loop(begin, segments[group * (STAGES + 1) + stage + 1], arrive, 0)

        @pl.when(s + 1 < blocks)
        def _():
            stream(s + 1).start()

        stream(s).wait()

        def batch(first, size):
            base = pl.multiple_of((group * listed + begin + first) * rows, rows)
            scores = lax.dot_general(
                held[pl.ds(base, size * rows), :],
                streamed[lax.rem(s, 2)],
                (((1,), (1,)), ((), ())),
                preferred_element_type=jnp.float32,
            )
            for p in range(size):
                one = scores[p * rows : (p + 1) * rows] * SCALE
                peak = jnp.max(one, axis=0, keepdims=True)
                lifted = jnp.exp2(one - peak)
                matrix[s, begin + first + p] = lifted
                peak_out[s, pl.ds(begin + first + p, 1), :] = peak
                sum_out[s, pl.ds(begin + first + p, 1), :] = jnp.sum(lifted, axis=0, keepdims=True)

        def four(q, carry):
            batch(4 * q, 4)
            return carry

        lax.fori_loop(0, live // 4, four, 0)
        for size in (1, 2, 3):
            pl.when(lax.rem(live, 4) == size)(functools.partial(batch, live - size, size))
        return carry

    lax.fori_loop(0, blocks, one_block, 0)
    if stage == STAGES - 1:
        for s in range(blocks):
            high = jnp.max(peak_out[s], axis=0, keepdims=True)
            high_out[s : s + 1, :] = high
            total_out[s : s + 1, :] = jnp.sum(sum_out[s] * jnp.exp2(peak_out[s] - high), axis=0, keepdims=True)


def score_stage(stage, listed, dest, segments, lives, source_vectors, pieces, earlier):
    blocks, block_rows, width = source_vectors.shape
    rows = pieces[0].shape[1]
    padded = 16
    hbm = pl.BlockSpec(memory_space=pltpu.HBM)
    vmem = pl.BlockSpec(memory_space=pltpu.VMEM)
    smem = pl.BlockSpec(memory_space=pltpu.SMEM)
    last = stage == STAGES - 1
    share = (0.25, 0.5, 0.25)[stage]
    small = jax.ShapeDtypeStruct((blocks, padded, block_rows), jnp.float32)
    whole = jax.ShapeDtypeStruct((blocks, block_rows), jnp.float32)
    if earlier:
        earlier = [pltpu.with_memory_space_constraint(earlier[0], pltpu.VMEM)] + earlier[1:]
    return pl.pallas_call(
        functools.partial(score_kernel, stage, listed),
        in_specs=[smem] * 3 + [hbm] * (1 + len(pieces)) + [vmem] * len(earlier),
        out_specs=[vmem] * (3 + 2 * last),
        out_shape=[pltpu.VMEM((blocks, listed, rows, block_rows), jnp.float32), small, small] + [whole] * 2 * last,
        scratch_shapes=[
            pltpu.VMEM((2 * listed * rows, width), jnp.bfloat16),
            pltpu.VMEM((2, block_rows, width), jnp.bfloat16),
            pltpu.SemaphoreType.DMA((2 * listed,)),
            pltpu.SemaphoreType.DMA((2,)),
        ],
        input_output_aliases={4 + len(pieces) + n: n for n in range(len(earlier))},
        compiler_params=pltpu.CompilerParams(vmem_limit_bytes=12 * MIB),
        cost_estimate=pl.CostEstimate(
            flops=int(2 * blocks * listed * rows * block_rows * width * share),
            bytes_accessed=int(4 * blocks * listed * rows * block_rows * share),
            transcendentals=0,
        ),
        name="scores",
    )(dest, segments, lives, source_vectors, *pieces, *earlier)


def column_kernel(final, counts, slots, order, level, part, near, far, back, matrix, peaks, *refs):
    sums_out = refs[0]
    weights, columns = refs[-2:]
    blocks, block_rows = part.shape
    listed, rows = matrix.shape[1:3]
    total = part[...] + near[...] + far[...] + back[...] + jnp.exp2(-level[...])
    inverse = 1.0 / total
    if final:
        refs[1][...] = -EPSILON * LN2 * (level[...] + jnp.log2(total))
    for s in range(blocks):
        weights[s] = jnp.exp2(peaks[s] - level[s : s + 1, :]) * inverse[s : s + 1, :]
    sums_out[...] = jnp.zeros_like(sums_out)
    lanes = block_rows // 128

    for g in range(blocks // SHARE):

        def one_entry(k, carry):
            def one_source(s, acc):
                w = weights[s, pl.ds(k, 1), :]
                spread = [jnp.broadcast_to(w[:, 128 * l : 128 * l + 128], (8, 128)) for l in range(lanes)]
                return tuple(
                    sum((matrix[s, k, 8 * j : 8 * j + 8, 128 * l : 128 * l + 128] * spread[l] for l in range(lanes)), a)
                    for j, a in enumerate(acc)
                )

            acc = tuple(jnp.zeros((8, 128), jnp.float32) for _ in range(rows // 8))
            for s in range(g * SHARE, (g + 1) * SHARE):
                live = order[(blocks + s) * listed + k] > 0
                acc = lax.cond(live, functools.partial(one_source, s), lambda acc: acc, acc)
            for j, a in enumerate(acc):
                columns[g * listed + k, 8 * j : 8 * j + 8, :] = a
            return carry

        lax.fori_loop(0, listed, one_entry, 0)

    lane = lax.broadcasted_iota(jnp.int32, (8, 128), 1)
    merged = [jnp.zeros((8, 128), jnp.float32)] * (rows // 8)
    for e in range(2 * listed):
        for j in range(rows // 8):
            one = jnp.sum(columns[e, 8 * j : 8 * j + 8, :], axis=1, keepdims=True)
            merged[j] = jnp.where(lane == e, one, merged[j])
    by_entry = jnp.concatenate(merged, axis=0).T
    for e in range(2 * listed):
        sums_out[pl.ds(slots[e], 1), :] = by_entry[e : e + 1, :]


def column_pass(final, counts, slots, order, targets, level, parts, matrix, peaks):
    blocks, block_rows = level.shape
    rows = matrix.shape[2]
    vmem = pl.BlockSpec(memory_space=pltpu.VMEM)
    smem = pl.BlockSpec(memory_space=pltpu.SMEM)
    out_shape = [jax.ShapeDtypeStruct((targets, rows), jnp.float32)]
    if final:
        out_shape.append(jax.ShapeDtypeStruct((blocks, block_rows), jnp.float32))
    return pl.pallas_call(
        functools.partial(column_kernel, final),
        in_specs=[smem] * 3 + [vmem] * 7,
        out_specs=[vmem] * len(out_shape),
        out_shape=out_shape,
        scratch_shapes=[
            pltpu.VMEM(peaks.shape, jnp.float32),
            pltpu.VMEM((2 * matrix.shape[1], rows, 128), jnp.float32),
        ],
        compiler_params=pltpu.CompilerParams(vmem_limit_bytes=8 * MIB),
        name="columns",
    )(counts, slots, order, level, *parts, matrix, peaks)


def row_kernel(counts, slots, order, level, sums, matrix, peaks, out, weights, gathered, spread):
    blocks, block_rows = out.shape
    listed, rows = matrix.shape[1:3]
    for e in range(2 * listed):
        gathered[e : e + 1, :] = sums[pl.ds(slots[e], 1), :]
    factors = (1.0 / (1.0 + gathered[...])).T
    for e in range(2 * listed):
        spread[e] = jnp.broadcast_to(factors[:, e : e + 1], (rows, 128))
    for s in range(blocks):
        weights[s] = jnp.exp2(peaks[s] - level[s : s + 1, :])
    lanes = block_rows // 128
    for s in range(blocks):
        g = s // SHARE

        def one_entry(t, total):
            k = order[s * listed + t]
            acc = [jnp.zeros((8, 128), jnp.float32) for _ in range(lanes)]
            for j in range(0, rows, 8):
                v = spread[g * listed + k, j : j + 8, :]
                for l in range(lanes):
                    acc[l] = acc[l] + matrix[s, k, j : j + 8, 128 * l : 128 * l + 128] * v
            w = weights[s, pl.ds(k, 1), :]
            return tuple(t + a * w[:, 128 * l : 128 * l + 128] for l, (t, a) in enumerate(zip(total, acc)))

        total = lax.fori_loop(
            0, counts[s], one_entry, tuple(jnp.zeros((8, 128), jnp.float32) for _ in range(lanes))
        )
        out[s : s + 1, :] = jnp.concatenate([jnp.sum(t, axis=0, keepdims=True) for t in total], axis=1)


def row_pass(counts, slots, order, level, sums, matrix, peaks):
    blocks, block_rows = level.shape
    listed, rows = matrix.shape[1:3]
    vmem = pl.BlockSpec(memory_space=pltpu.VMEM)
    smem = pl.BlockSpec(memory_space=pltpu.SMEM)
    return pl.pallas_call(
        row_kernel,
        in_specs=[smem] * 3 + [vmem] * 4,
        out_specs=vmem,
        out_shape=jax.ShapeDtypeStruct((blocks, block_rows), jnp.float32),
        scratch_shapes=[
            pltpu.VMEM(peaks.shape, jnp.float32),
            pltpu.VMEM((128, rows), jnp.float32),
            pltpu.VMEM((2 * listed, rows, 128), jnp.float32),
        ],
        compiler_params=pltpu.CompilerParams(vmem_limit_bytes=8 * MIB),
        name="rows",
    )(counts, slots, order, level, sums, matrix, peaks)


def from_columns(x):
    return [x] + [lax.ppermute(x, "col", [(i, (i + d) % 4) for i in range(4)]) for d in (1, 2, 3)]


def sum_over_rows(x):
    x = x + send(x, 0, 0, 1)
    x = x + send(x, 0, 1, 0) + send(x, 0, 2, 0) + send(x, 0, 3, 0)
    return x + send(x, 1, 0, 0) + send(x, 2, 0, 0) + send(x, 3, 0, 0)


def tables_kernel(target_blocks, me, pairs, counts, owners, slots, dest, segments, lives, order, listing):
    blocks, listed = pairs.shape
    starts = np.cumsum([0] + [len(stage) for stage in piece_layout()])
    z, y, core = me[0] // 8, (me[0] // 2) % 4, me[0] % 2
    for n in range(int(starts[-1])):
        dest[n] = -1
    for g in range(blocks // SHARE):
        found = []
        for k in range(listed):
            slot = owners[pairs[g * SHARE, k]]
            owner, which = slot // target_blocks, slot % target_blocks
            dz = (owner // 8 - z + 4) % 4
            dy = ((owner // 2) % 4 - y + 4) % 4
            other = jnp.where(owner % 2 == core, 0, 1)
            across = jnp.where(which == 0, dz, dy)
            along = jnp.where(which == 0, dy, dz)
            stage = jnp.where(across == 0, 0, jnp.where(across == 2, 2, 1))
            index = jnp.where(along == 0, 0, jnp.where(along == 3, 1, along + 1))
            set_at = other * 2 + which
            near = 2 * set_at + jnp.where(across == 3, 0, 1)
            position = index + 4 * jnp.where(stage == 1, near, set_at)
            base = jnp.where(stage == 0, int(starts[0]), jnp.where(stage == 1, int(starts[1]), int(starts[2])))
            found.append((slot, stage, base + position))
        following = []
        begin = jnp.int32(0)
        for stage in range(STAGES):
            segments[g * (STAGES + 1) + stage] = begin
            following.append(begin)
            begin = begin + sum(jnp.where(f[1] == stage, 1, 0) for f in found)
        segments[g * (STAGES + 1) + STAGES] = begin
        for k, (slot, stage, position) in enumerate(found):
            place = jnp.where(stage == 0, following[0], jnp.where(stage == 1, following[1], following[2]))
            following = [f + jnp.where(stage == n, 1, 0) for n, f in enumerate(following)]
            slots[g * listed + place] = slot
            dest[position] = g * listed + place
            listing[place] = k
        for s in range(g * SHARE, (g + 1) * SHARE):
            count = counts[s]
            for stage in range(STAGES):
                lives[s * STAGES + stage] = sum(
                    jnp.where((f[1] == stage) & (k < count), 1, 0) for k, f in enumerate(found)
                )
            turn = jnp.int32(0)
            for place in range(listed):
                live = jnp.where(listing[place] < count, 1, 0)
                order[s * listed + turn] = place
                order[(blocks + s) * listed + place] = live
                turn = turn + live


def tables(pair_list, counts, owner_map, target_blocks):
    blocks, listed = pair_list.shape
    entries = blocks // SHARE * listed
    me = jnp.reshape(lax.axis_index("row"), (1,)).astype(jnp.int32)
    smem = pl.BlockSpec(memory_space=pltpu.SMEM)
    sizes = (entries, owner_map.shape[0], blocks // SHARE * (STAGES + 1), blocks * STAGES, 2 * blocks * listed)
    return pl.pallas_call(
        functools.partial(tables_kernel, target_blocks),
        in_specs=[smem] * 4,
        out_specs=[smem] * 5,
        out_shape=[jax.ShapeDtypeStruct((size,), jnp.int32) for size in sizes],
        scratch_shapes=[pltpu.SMEM((listed,), jnp.int32)],
        name="tables",
    )(me, pair_list, counts, owner_map)


def shards(source_vectors, target_vectors, pair_list, counts, owner_map):
    target_blocks, quarter, _ = target_vectors.shape
    listed = pair_list.shape[1]
    targets = owner_map.shape[0]
    source_vectors = pltpu.with_memory_space_constraint(source_vectors, pltpu.HBM)
    slots, dest, segments, lives, order = tables(pair_list, counts, owner_map, target_blocks)

    def across(pieces):
        pieces = pieces + [send(piece, 0, 0, 1) for piece in pieces]
        return [pltpu.with_memory_space_constraint(piece, pltpu.HBM) for piece in pieces]

    def stage(number, pieces, earlier):
        return score_stage(
            number, listed, dest, segments, lives, source_vectors, across(pieces), earlier
        )

    along_y, along_z = target_vectors[:1], target_vectors[1:]
    arrived = ring_sends(along_y, 0, 1) + ring_sends(along_z, 1, 0)
    *arrived, slots, dest, segments, lives, order = tie(*arrived, slots, dest, segments, lives, order)
    first = [jnp.concatenate([along_y] + arrived[:3], axis=0), jnp.concatenate([along_z] + arrived[3:], axis=0)]
    second = [
        send(first[0], 1, 0, 0),
        send(first[0], -1, 0, 0),
        send(first[1], 0, 1, 0),
        send(first[1], 0, -1, 0),
    ]
    done = stage(0, first, [])
    *second, peaks = tie(*second, done[1])
    third = [
        send(second[0][:2], 1, 0, 0),
        send(second[1][2:], -1, 0, 0),
        send(second[2][:2], 0, 1, 0),
        send(second[3][2:], 0, -1, 0),
    ]
    done = stage(1, second, [done[0], peaks, done[2]])
    *third, peaks = tie(*third, done[1])
    matrix, peaks, _, high, total = stage(2, third, [done[0], peaks, done[2]])
    matrix = pltpu.with_memory_space_constraint(matrix, pltpu.VMEM)

    both = from_columns(jnp.stack([high, total]))
    level = jnp.maximum(functools.reduce(jnp.maximum, [b[0] for b in both]), 0.0)
    parts = [b[1] * jnp.exp2(b[0] - level) for b in both]

    for sweep_index in range(SWEEPS):
        final = sweep_index == SWEEPS - 1
        sums = column_pass(final, counts, slots, order, targets, level, parts, matrix, peaks)
        if final:
            break
        sums = sum_over_rows(sums[0])
        parts = from_columns(row_pass(counts, slots, order, level, sums, matrix, peaks))
    sums, source_dual = sums
    row_count = targets // target_blocks
    back = lax.all_to_all(
        sums.reshape(row_count, target_blocks, quarter), "row", split_axis=0, concat_axis=0, tiled=True
    )
    target_dual = -EPSILON * jnp.log(1.0 + jnp.sum(back, axis=0))
    return source_dual, target_dual


def solution(mesh):
    return jax.shard_map(
        shards,
        mesh=mesh,
        in_specs=(P("row", None, None), P("row", "col", None), P("row", None), P("row"), P()),
        out_specs=(P("row", None), P("row", "col")),
        check_vma=False,
    )
```

```python
import functools

import jax
import jax.numpy as jnp
import numpy as np
from jax import lax
from jax.experimental import pallas as pl
from jax.experimental.pallas import tpu as pltpu
from jax.sharding import PartitionSpec as P

SHARE = 4
SWEEPS = 3
EPSILON = 0.05
LOG2E = 1.4426950408889634
LN2 = 0.6931471805599453
SCALE = LOG2E / EPSILON
NEGATIVE = -1e30
MIB = 2**20


def row_perm(dz, dy, dc):
    return [
        ((z * 4 + y) * 2 + c, (((z + dz) % 4) * 4 + (y + dy) % 4) * 2 + (c ^ dc))
        for z in range(4)
        for y in range(4)
        for c in range(2)
    ]


def send(x, dz, dy, dc):
    return lax.ppermute(x, "row", row_perm(dz, dy, dc))


RING = (0, -1, 1, 2)
STAGES = 3


def tie(*arrays):
    return lax.optimization_barrier(arrays)


def ring_sends(own, dz, dy):
    return [send(own, dz, dy, 0), send(own, -dz, -dy, 0), send(own, 2 * dz, 2 * dy, 0)]


def piece_layout():
    first = [(core, which, 0, RING) for core in range(2) for which in range(2)]
    second = [(core, which, d, RING) for core in range(2) for which in range(2) for d in (-1, 1)]
    third = [
        (core, which, 2, half) for core in range(2) for which in range(2) for half in (RING[:2], RING[2:])
    ]
    stages = []
    for pieces in (first, second, third):
        entries = []
        for piece, (core, which, across, ring) in enumerate(pieces):
            for index, along in enumerate(ring):
                dz, dy = (across, along) if which == 0 else (along, across)
                entries.append((piece, index, dz, dy, core, which))
        stages.append(entries)
    return stages


SLOTS, DEST, SEGMENTS, LIVES, ORDER, ALIVE, COUNTS, TABLE = 0, 24, 88, 96, 120, 216, 312, 320


def score_kernel(stage, listed, table, source, *refs):
    layout = piece_layout()[stage]
    number = max(entry[0] for entry in layout) + 1
    pieces, refs = refs[:number], refs[number:]
    if stage > 0:
        refs = refs[3:]
    matrix, peak_out, sum_out = refs[:3]
    if stage == STAGES - 1:
        high_out, total_out = refs[3:5]
    held, fetch_sems = refs[-2:]
    blocks = source.shape[0]
    rows = matrix.shape[2]

    def stream(s):
        return pltpu.make_async_copy(source.at[s], streamed.at[lax.rem(s, 2)], stream_sems.at[lax.rem(s, 2)])


    def fetch(piece, index, entry):
        return pltpu.make_async_copy(
            pieces[piece].at[index], held.at[pl.ds(entry * rows, rows)], fetch_sems.at[entry]
        )

    offset = DEST + sum(len(entries) for entries in piece_layout()[:stage])
    for position, (piece, index, *_) in enumerate(layout, offset):

        @pl.when(table[position] >= 0)
        def _():
            fetch(piece, index, table[position]).start()

    if stage == 0:
        peak_out[...] = jnp.full(peak_out.shape, NEGATIVE, jnp.float32)
        sum_out[...] = jnp.zeros(sum_out.shape, jnp.float32)

    def one_block(s, carry):
        group = s // SHARE
        begin = table[SEGMENTS + group * (STAGES + 1) + stage]
        live = table[LIVES + s * STAGES + stage]

        @pl.when(lax.rem(s, SHARE) == 0)
        def _():
            def arrive(entry, carry):
                fetch(0, 0, group * listed + entry).wait()
                return carry

            lax.fori_loop(begin, table[SEGMENTS + group * (STAGES + 1) + stage + 1], arrive, 0)

        def batch(first, size):
            base = pl.multiple_of((group * listed + begin + first) * rows, rows)
            scores = lax.dot_general(
                held[pl.ds(base, size * rows), :],
                source[s],
                (((1,), (1,)), ((), ())),
                preferred_element_type=jnp.float32,
            )
            for p in range(size):
                one = scores[p * rows : (p + 1) * rows] * SCALE
                peak = jnp.max(one, axis=0, keepdims=True)
                lifted = jnp.exp2(one - peak)
                matrix[s, begin + first + p] = lifted
                peak_out[s, pl.ds(begin + first + p, 1), :] = peak
                sum_out[s, pl.ds(begin + first + p, 1), :] = jnp.sum(lifted, axis=0, keepdims=True)

        def four(q, carry):
            batch(4 * q, 4)
            return carry

        lax.fori_loop(0, live // 4, four, 0)
        for size in (1, 2, 3):
            pl.when(lax.rem(live, 4) == size)(functools.partial(batch, live - size, size))
        return carry

    lax.fori_loop(0, blocks, one_block, 0)
    if stage == STAGES - 1:
        for s in range(blocks):
            high = jnp.max(peak_out[s], axis=0, keepdims=True)
            high_out[s : s + 1, :] = high
            total_out[s : s + 1, :] = jnp.sum(sum_out[s] * jnp.exp2(peak_out[s] - high), axis=0, keepdims=True)


def score_stage(stage, listed, table, source_vectors, pieces, earlier):
    blocks, block_rows, width = source_vectors.shape
    rows = pieces[0].shape[1]
    padded = 16
    hbm = pl.BlockSpec(memory_space=pltpu.HBM)
    vmem = pl.BlockSpec(memory_space=pltpu.VMEM)
    smem = pl.BlockSpec(memory_space=pltpu.SMEM)
    last = stage == STAGES - 1
    share = (0.25, 0.5, 0.25)[stage]
    small = jax.ShapeDtypeStruct((blocks, padded, block_rows), jnp.float32)
    whole = jax.ShapeDtypeStruct((blocks, block_rows), jnp.float32)
    if earlier:
        earlier = [pltpu.with_memory_space_constraint(earlier[0], pltpu.VMEM)] + earlier[1:]
    return pl.pallas_call(
        functools.partial(score_kernel, stage, listed),
        in_specs=[smem, vmem] + [hbm] * len(pieces) + [vmem] * len(earlier),
        out_specs=[vmem] * (3 + 2 * last),
        out_shape=[pltpu.VMEM((blocks, listed, rows, block_rows), jnp.float32), small, small] + [whole] * 2 * last,
        scratch_shapes=[
            pltpu.VMEM((2 * listed * rows, width), jnp.bfloat16),
            pltpu.SemaphoreType.DMA((2 * listed,)),
        ],
        input_output_aliases={2 + len(pieces) + n: n for n in range(len(earlier))},
        compiler_params=pltpu.CompilerParams(vmem_limit_bytes=8 * MIB),
        cost_estimate=pl.CostEstimate(
            flops=int(2 * blocks * listed * rows * block_rows * width * share),
            bytes_accessed=int(4 * blocks * listed * rows * block_rows * share),
            transcendentals=0,
        ),
        name="scores",
    )(table, source_vectors, *pieces, *earlier)


def column_kernel(final, table, level, part, near, far, back, matrix, peaks, *refs):
    sums_out = refs[0]
    weights, columns = refs[-2:]
    blocks, block_rows = part.shape
    listed, rows = matrix.shape[1:3]
    total = part[...] + near[...] + far[...] + back[...] + jnp.exp2(-level[...])
    inverse = 1.0 / total
    if final:
        refs[1][...] = -EPSILON * LN2 * (level[...] + jnp.log2(total))
    for s in range(blocks):
        weights[s] = jnp.exp2(peaks[s] - level[s : s + 1, :]) * inverse[s : s + 1, :]
    sums_out[...] = jnp.zeros_like(sums_out)
    lanes = block_rows // 128

    for g in range(blocks // SHARE):

        def one_entry(k, carry):
            def one_source(s, acc):
                w = weights[s, pl.ds(k, 1), :]
                spread = [jnp.broadcast_to(w[:, 128 * l : 128 * l + 128], (8, 128)) for l in range(lanes)]
                return tuple(
                    sum((matrix[s, k, 8 * j : 8 * j + 8, 128 * l : 128 * l + 128] * spread[l] for l in range(lanes)), a)
                    for j, a in enumerate(acc)
                )

            acc = tuple(jnp.zeros((8, 128), jnp.float32) for _ in range(rows // 8))
            for s in range(g * SHARE, (g + 1) * SHARE):
                live = table[ALIVE + s * listed + k] > 0
                acc = lax.cond(live, functools.partial(one_source, s), lambda acc: acc, acc)
            for j, a in enumerate(acc):
                columns[g * listed + k, 8 * j : 8 * j + 8, :] = a
            return carry

        lax.fori_loop(0, listed, one_entry, 0)

    lane = lax.broadcasted_iota(jnp.int32, (8, 128), 1)
    merged = [jnp.zeros((8, 128), jnp.float32)] * (rows // 8)
    for e in range(2 * listed):
        for j in range(rows // 8):
            one = jnp.sum(columns[e, 8 * j : 8 * j + 8, :], axis=1, keepdims=True)
            merged[j] = jnp.where(lane == e, one, merged[j])
    by_entry = jnp.concatenate(merged, axis=0).T
    for e in range(2 * listed):
        sums_out[pl.ds(table[SLOTS + e], 1), :] = by_entry[e : e + 1, :]


def column_pass(final, table, targets, level, parts, matrix, peaks):
    blocks, block_rows = level.shape
    rows = matrix.shape[2]
    vmem = pl.BlockSpec(memory_space=pltpu.VMEM)
    smem = pl.BlockSpec(memory_space=pltpu.SMEM)
    out_shape = [jax.ShapeDtypeStruct((targets, rows), jnp.float32)]
    if final:
        out_shape.append(jax.ShapeDtypeStruct((blocks, block_rows), jnp.float32))
    return pl.pallas_call(
        functools.partial(column_kernel, final),
        in_specs=[smem] + [vmem] * 7,
        out_specs=[vmem] * len(out_shape),
        out_shape=out_shape,
        scratch_shapes=[
            pltpu.VMEM(peaks.shape, jnp.float32),
            pltpu.VMEM((2 * matrix.shape[1], rows, 128), jnp.float32),
        ],
        compiler_params=pltpu.CompilerParams(vmem_limit_bytes=8 * MIB),
        name="columns",
    )(table, level, *parts, matrix, peaks)


def row_kernel(table, level, sums, matrix, peaks, out, weights, gathered, spread):
    blocks, block_rows = out.shape
    listed, rows = matrix.shape[1:3]
    for e in range(2 * listed):
        gathered[e : e + 1, :] = sums[pl.ds(table[SLOTS + e], 1), :]
    factors = (1.0 / (1.0 + gathered[...])).T
    for e in range(2 * listed):
        spread[e] = jnp.broadcast_to(factors[:, e : e + 1], (rows, 128))
    for s in range(blocks):
        weights[s] = jnp.exp2(peaks[s] - level[s : s + 1, :])
    lanes = block_rows // 128
    for s in range(blocks):
        g = s // SHARE

        def one_entry(t, total):
            k = table[ORDER + s * listed + t]
            acc = [jnp.zeros((8, 128), jnp.float32) for _ in range(lanes)]
            for j in range(0, rows, 8):
                v = spread[g * listed + k, j : j + 8, :]
                for l in range(lanes):
                    acc[l] = acc[l] + matrix[s, k, j : j + 8, 128 * l : 128 * l + 128] * v
            w = weights[s, pl.ds(k, 1), :]
            return tuple(t + a * w[:, 128 * l : 128 * l + 128] for l, (t, a) in enumerate(zip(total, acc)))

        total = lax.fori_loop(
            0, table[COUNTS + s], one_entry, tuple(jnp.zeros((8, 128), jnp.float32) for _ in range(lanes))
        )
        out[s : s + 1, :] = jnp.concatenate([jnp.sum(t, axis=0, keepdims=True) for t in total], axis=1)


def row_pass(table, level, sums, matrix, peaks):
    blocks, block_rows = level.shape
    listed, rows = matrix.shape[1:3]
    vmem = pl.BlockSpec(memory_space=pltpu.VMEM)
    smem = pl.BlockSpec(memory_space=pltpu.SMEM)
    return pl.pallas_call(
        row_kernel,
        in_specs=[smem] + [vmem] * 4,
        out_specs=vmem,
        out_shape=jax.ShapeDtypeStruct((blocks, block_rows), jnp.float32),
        scratch_shapes=[
            pltpu.VMEM(peaks.shape, jnp.float32),
            pltpu.VMEM((128, rows), jnp.float32),
            pltpu.VMEM((2 * listed, rows, 128), jnp.float32),
        ],
        compiler_params=pltpu.CompilerParams(vmem_limit_bytes=8 * MIB),
        name="rows",
    )(table, level, sums, matrix, peaks)


def from_columns(x):
    return [x] + [lax.ppermute(x, "col", [(i, (i + d) % 4) for i in range(4)]) for d in (1, 2, 3)]


def sum_over_rows(x):
    x = x + send(x, 0, 0, 1)
    x = x + send(x, 0, 1, 0) + send(x, 0, 2, 0) + send(x, 0, 3, 0)
    return x + send(x, 1, 0, 0) + send(x, 2, 0, 0) + send(x, 3, 0, 0)


def tables_kernel(target_blocks, me, pairs, counts, owners, source, table, loaded, listing, sems):
    blocks, listed = pairs.shape
    copies = [pltpu.make_async_copy(source.at[s], loaded.at[s], sems.at[s]) for s in range(blocks)]
    for copy in copies:
        copy.start()
    starts = np.cumsum([0] + [len(stage) for stage in piece_layout()])
    z, y, core = me[0] // 8, (me[0] // 2) % 4, me[0] % 2
    for n in range(int(starts[-1])):
        table[DEST + n] = -1
    for g in range(blocks // SHARE):
        found = []
        for k in range(listed):
            slot = owners[pairs[g * SHARE, k]]
            owner, which = slot // target_blocks, slot % target_blocks
            dz = (owner // 8 - z + 4) % 4
            dy = ((owner // 2) % 4 - y + 4) % 4
            other = jnp.where(owner % 2 == core, 0, 1)
            across = jnp.where(which == 0, dz, dy)
            along = jnp.where(which == 0, dy, dz)
            stage = jnp.where(across == 0, 0, jnp.where(across == 2, 2, 1))
            index = jnp.where(along == 0, 0, jnp.where(along == 3, 1, along + 1))
            set_at = other * 2 + which
            near = 2 * set_at + jnp.where(across == 3, 0, 1)
            position = index + 4 * jnp.where(stage == 1, near, set_at)
            base = jnp.where(stage == 0, int(starts[0]), jnp.where(stage == 1, int(starts[1]), int(starts[2])))
            found.append((slot, stage, base + position))
        following = []
        begin = jnp.int32(0)
        for stage in range(STAGES):
            table[SEGMENTS + g * (STAGES + 1) + stage] = begin
            following.append(begin)
            begin = begin + sum(jnp.where(f[1] == stage, 1, 0) for f in found)
        table[SEGMENTS + g * (STAGES + 1) + STAGES] = begin
        for k, (slot, stage, position) in enumerate(found):
            place = jnp.where(stage == 0, following[0], jnp.where(stage == 1, following[1], following[2]))
            following = [f + jnp.where(stage == n, 1, 0) for n, f in enumerate(following)]
            table[SLOTS + g * listed + place] = slot
            table[DEST + position] = g * listed + place
            listing[place] = k
        for s in range(g * SHARE, (g + 1) * SHARE):
            count = counts[s]
            table[COUNTS + s] = count
            for stage in range(STAGES):
                table[LIVES + s * STAGES + stage] = sum(
                    jnp.where((f[1] == stage) & (k < count), 1, 0) for k, f in enumerate(found)
                )
            turn = jnp.int32(0)
            for place in range(listed):
                live = jnp.where(listing[place] < count, 1, 0)
                table[ORDER + s * listed + turn] = place
                table[ALIVE + s * listed + place] = live
                turn = turn + live
    for copy in copies:
        copy.wait()


def tables(pair_list, counts, owner_map, source_vectors, target_blocks):
    listed = pair_list.shape[1]
    me = jnp.reshape(lax.axis_index("row"), (1,)).astype(jnp.int32)
    smem = pl.BlockSpec(memory_space=pltpu.SMEM)
    return pl.pallas_call(
        functools.partial(tables_kernel, target_blocks),
        in_specs=[smem] * 4 + [pl.BlockSpec(memory_space=pltpu.HBM)],
        out_specs=[smem, pl.BlockSpec(memory_space=pltpu.VMEM)],
        out_shape=[
            jax.ShapeDtypeStruct((TABLE,), jnp.int32),
            pltpu.VMEM(source_vectors.shape, source_vectors.dtype),
        ],
        scratch_shapes=[pltpu.SMEM((listed,), jnp.int32), pltpu.SemaphoreType.DMA(source_vectors.shape[:1])],
        compiler_params=pltpu.CompilerParams(vmem_limit_bytes=4 * MIB),
        name="tables",
    )(me, pair_list, counts, owner_map, source_vectors)


def shards(source_vectors, target_vectors, pair_list, counts, owner_map):
    target_blocks, quarter, _ = target_vectors.shape
    listed = pair_list.shape[1]
    targets = owner_map.shape[0]
    source_vectors = pltpu.with_memory_space_constraint(source_vectors, pltpu.HBM)
    table, loaded = tables(pair_list, counts, owner_map, source_vectors, target_blocks)

    def stage(number, pieces, earlier):
        pieces = pieces + [send(piece, 0, 0, 1) for piece in pieces]
        pieces = [pltpu.with_memory_space_constraint(piece, pltpu.HBM) for piece in pieces]
        return score_stage(number, listed, table, loaded, pieces, earlier)

    along_y, along_z = target_vectors[:1], target_vectors[1:]
    arrived = ring_sends(along_y, 0, 1) + ring_sends(along_z, 1, 0)
    *arrived, table, loaded = tie(*arrived, table, loaded)
    loaded = pltpu.with_memory_space_constraint(loaded, pltpu.VMEM)
    first = [jnp.concatenate([along_y] + arrived[:3], axis=0), jnp.concatenate([along_z] + arrived[3:], axis=0)]
    second = [
        send(first[0], 1, 0, 0),
        send(first[0], -1, 0, 0),
        send(first[1], 0, 1, 0),
        send(first[1], 0, -1, 0),
    ]
    done = stage(0, first, [])
    *second, peaks = tie(*second, done[1])
    third = [
        send(second[0][:2], 1, 0, 0),
        send(second[1][2:], -1, 0, 0),
        send(second[2][:2], 0, 1, 0),
        send(second[3][2:], 0, -1, 0),
    ]
    done = stage(1, second, [done[0], peaks, done[2]])
    *third, peaks = tie(*third, done[1])
    matrix, peaks, _, high, total = stage(2, third, [done[0], peaks, done[2]])
    matrix = pltpu.with_memory_space_constraint(matrix, pltpu.VMEM)

    both = from_columns(jnp.stack([high, total]))
    level = jnp.maximum(functools.reduce(jnp.maximum, [b[0] for b in both]), 0.0)
    parts = [b[1] * jnp.exp2(b[0] - level) for b in both]

    for sweep_index in range(SWEEPS):
        final = sweep_index == SWEEPS - 1
        sums = column_pass(final, table, targets, level, parts, matrix, peaks)
        if final:
            break
        sums = sum_over_rows(sums[0])
        parts = from_columns(row_pass(table, level, sums, matrix, peaks))
    sums, source_dual = sums
    row_count = targets // target_blocks
    back = lax.all_to_all(
        sums.reshape(row_count, target_blocks, quarter), "row", split_axis=0, concat_axis=0, tiled=True
    )
    target_dual = -EPSILON * jnp.log(1.0 + jnp.sum(back, axis=0))
    return source_dual, target_dual


def solution(mesh):
    return jax.shard_map(
        shards,
        mesh=mesh,
        in_specs=(P("row", None, None), P("row", "col", None), P("row", None), P("row"), P()),
        out_specs=(P("row", None), P("row", "col")),
        check_vma=False,
    )
```

```python
import functools

import jax
import jax.numpy as jnp
import numpy as np
from jax import lax
from jax.experimental import pallas as pl
from jax.experimental.pallas import tpu as pltpu
from jax.sharding import PartitionSpec as P

SHARE = 4
SWEEPS = 3
EPSILON = 0.05
LOG2E = 1.4426950408889634
LN2 = 0.6931471805599453
SCALE = LOG2E / EPSILON
NEGATIVE = -1e30
MIB = 2**20


def row_perm(dz, dy, dc):
    return [
        ((z * 4 + y) * 2 + c, (((z + dz) % 4) * 4 + (y + dy) % 4) * 2 + (c ^ dc))
        for z in range(4)
        for y in range(4)
        for c in range(2)
    ]


def send(x, dz, dy, dc):
    return lax.ppermute(x, "row", row_perm(dz, dy, dc))


RING = (0, -1, 1, 2)
STAGES = 3
TOGETHER = (1, 2, 4)


def tie(*arrays):
    return lax.optimization_barrier(arrays)


def ring_sends(own, dz, dy):
    return [send(own, dz, dy, 0), send(own, -dz, -dy, 0), send(own, 2 * dz, 2 * dy, 0)]


def piece_layout():
    first = [(core, which, 0, RING) for core in range(2) for which in range(2)]
    second = [(core, which, d, RING) for core in range(2) for which in range(2) for d in (-1, 1)]
    third = [
        (core, which, 2, half) for core in range(2) for which in range(2) for half in (RING[:2], RING[2:])
    ]
    stages = []
    for pieces in (first, second, third):
        entries = []
        for piece, (core, which, across, ring) in enumerate(pieces):
            for index, along in enumerate(ring):
                dz, dy = (across, along) if which == 0 else (along, across)
                entries.append((piece, index, dz, dy, core, which))
        stages.append(entries)
    return stages


SLOTS, DEST, SEGMENTS, LIVES, ORDER, ALIVE, COUNTS, TABLE = 0, 24, 88, 96, 120, 216, 312, 320


def score_kernel(stage, listed, table, source, *refs):
    layout = piece_layout()[stage]
    number = max(entry[0] for entry in layout) + 1
    pieces, refs = refs[:number], refs[number:]
    if stage > 0:
        refs = refs[3:]
    matrix, peak_out, sum_out = refs[:3]
    if stage == STAGES - 1:
        high_out, total_out = refs[3:5]
    held, fetch_sems = refs[-2:]
    blocks = source.shape[0]
    rows = matrix.shape[2]

    def stream(s):
        return pltpu.make_async_copy(source.at[s], streamed.at[lax.rem(s, 2)], stream_sems.at[lax.rem(s, 2)])


    def fetch(piece, index, entry):
        return pltpu.make_async_copy(
            pieces[piece].at[index], held.at[pl.ds(entry * rows, rows)], fetch_sems.at[entry]
        )

    offset = DEST + sum(len(entries) for entries in piece_layout()[:stage])
    for position, (piece, index, *_) in enumerate(layout, offset):

        @pl.when(table[position] >= 0)
        def _():
            fetch(piece, index, table[position]).start()

    if stage == 0:
        peak_out[...] = jnp.full(peak_out.shape, NEGATIVE, jnp.float32)
        sum_out[...] = jnp.zeros(sum_out.shape, jnp.float32)

    together = TOGETHER[stage]
    largest = 8 // together if together > 1 else 4

    def some_blocks(turn, carry):
        group = turn * together // SHARE
        begin = table[SEGMENTS + group * (STAGES + 1) + stage]
        alive = [table[LIVES + (turn * together + m) * STAGES + stage] for m in range(together)]
        live = functools.reduce(jnp.maximum, alive)

        @pl.when(lax.rem(turn * together, SHARE) == 0)
        def _():
            def arrive(entry, carry):
                fetch(0, 0, group * listed + entry).wait()
                return carry

            lax.fori_loop(begin, table[SEGMENTS + group * (STAGES + 1) + stage + 1], arrive, 0)

        def batch(first, size):
            base = pl.multiple_of((group * listed + begin + first) * rows, rows)
            vectors = held[pl.ds(base, size * rows), :]
            scores = [
                lax.dot_general(
                    vectors,
                    source[turn * together + m],
                    (((1,), (1,)), ((), ())),
                    preferred_element_type=jnp.float32,
                )
                for m in range(together)
            ]
            for m in range(together):
                s = turn * together + m
                for p in range(size):
                    one = scores[m][p * rows : (p + 1) * rows] * SCALE
                    peak = jnp.max(one, axis=0, keepdims=True)
                    lifted = jnp.exp2(one - peak)
                    matrix[s, begin + first + p] = lifted
                    total = jnp.sum(lifted, axis=0, keepdims=True)
                    if together > 1:
                        used = first + p < alive[m]
                        peak, total = jnp.where(used, peak, NEGATIVE), jnp.where(used, total, 0.0)
                    peak_out[s, pl.ds(begin + first + p, 1), :] = peak
                    sum_out[s, pl.ds(begin + first + p, 1), :] = total

        def whole(q, carry):
            batch(largest * q, largest)
            return carry

        lax.fori_loop(0, live // largest, whole, 0)
        for size in range(1, largest):
            pl.when(lax.rem(live, largest) == size)(functools.partial(batch, live - size, size))
        return carry

    lax.fori_loop(0, blocks // together, some_blocks, 0)
    if stage == STAGES - 1:
        for s in range(blocks):
            high = jnp.max(peak_out[s], axis=0, keepdims=True)
            high_out[s : s + 1, :] = high
            total_out[s : s + 1, :] = jnp.sum(sum_out[s] * jnp.exp2(peak_out[s] - high), axis=0, keepdims=True)


def score_stage(stage, listed, table, source_vectors, pieces, earlier):
    blocks, block_rows, width = source_vectors.shape
    rows = pieces[0].shape[1]
    padded = 16
    hbm = pl.BlockSpec(memory_space=pltpu.HBM)
    vmem = pl.BlockSpec(memory_space=pltpu.VMEM)
    smem = pl.BlockSpec(memory_space=pltpu.SMEM)
    last = stage == STAGES - 1
    share = (0.25, 0.5, 0.25)[stage]
    small = jax.ShapeDtypeStruct((blocks, padded, block_rows), jnp.float32)
    whole = jax.ShapeDtypeStruct((blocks, block_rows), jnp.float32)
    if earlier:
        earlier = [pltpu.with_memory_space_constraint(earlier[0], pltpu.VMEM)] + earlier[1:]
    return pl.pallas_call(
        functools.partial(score_kernel, stage, listed),
        in_specs=[smem, vmem] + [hbm] * len(pieces) + [vmem] * len(earlier),
        out_specs=[vmem] * (3 + 2 * last),
        out_shape=[pltpu.VMEM((blocks, listed, rows, block_rows), jnp.float32), small, small] + [whole] * 2 * last,
        scratch_shapes=[
            pltpu.VMEM((2 * listed * rows, width), jnp.bfloat16),
            pltpu.SemaphoreType.DMA((2 * listed,)),
        ],
        input_output_aliases={2 + len(pieces) + n: n for n in range(len(earlier))},
        compiler_params=pltpu.CompilerParams(vmem_limit_bytes=8 * MIB),
        cost_estimate=pl.CostEstimate(
            flops=int(2 * blocks * listed * rows * block_rows * width * share),
            bytes_accessed=int(4 * blocks * listed * rows * block_rows * share),
            transcendentals=0,
        ),
        name="scores",
    )(table, source_vectors, *pieces, *earlier)


def column_kernel(final, table, level, part, near, far, back, matrix, peaks, *refs):
    sums_out = refs[0]
    weights, columns = refs[-2:]
    blocks, block_rows = part.shape
    listed, rows = matrix.shape[1:3]
    total = part[...] + near[...] + far[...] + back[...] + jnp.exp2(-level[...])
    inverse = 1.0 / total
    if final:
        refs[1][...] = -EPSILON * LN2 * (level[...] + jnp.log2(total))
    for s in range(blocks):
        weights[s] = jnp.exp2(peaks[s] - level[s : s + 1, :]) * inverse[s : s + 1, :]
    sums_out[...] = jnp.zeros_like(sums_out)
    lanes = block_rows // 128

    for g in range(blocks // SHARE):

        def one_entry(k, carry):
            def one_source(s, acc):
                w = weights[s, pl.ds(k, 1), :]
                spread = [jnp.broadcast_to(w[:, 128 * l : 128 * l + 128], (8, 128)) for l in range(lanes)]
                return tuple(
                    sum((matrix[s, k, 8 * j : 8 * j + 8, 128 * l : 128 * l + 128] * spread[l] for l in range(lanes)), a)
                    for j, a in enumerate(acc)
                )

            acc = tuple(jnp.zeros((8, 128), jnp.float32) for _ in range(rows // 8))
            for s in range(g * SHARE, (g + 1) * SHARE):
                live = table[ALIVE + s * listed + k] > 0
                acc = lax.cond(live, functools.partial(one_source, s), lambda acc: acc, acc)
            for j, a in enumerate(acc):
                columns[g * listed + k, 8 * j : 8 * j + 8, :] = a
            return carry

        lax.fori_loop(0, listed, one_entry, 0)

    lane = lax.broadcasted_iota(jnp.int32, (8, 128), 1)
    merged = [jnp.zeros((8, 128), jnp.float32)] * (rows // 8)
    for e in range(2 * listed):
        for j in range(rows // 8):
            one = jnp.sum(columns[e, 8 * j : 8 * j + 8, :], axis=1, keepdims=True)
            merged[j] = jnp.where(lane == e, one, merged[j])
    by_entry = jnp.concatenate(merged, axis=0).T
    for e in range(2 * listed):
        sums_out[pl.ds(table[SLOTS + e], 1), :] = by_entry[e : e + 1, :]


def column_pass(final, table, targets, level, parts, matrix, peaks):
    blocks, block_rows = level.shape
    rows = matrix.shape[2]
    vmem = pl.BlockSpec(memory_space=pltpu.VMEM)
    smem = pl.BlockSpec(memory_space=pltpu.SMEM)
    out_shape = [jax.ShapeDtypeStruct((targets, rows), jnp.float32)]
    if final:
        out_shape.append(jax.ShapeDtypeStruct((blocks, block_rows), jnp.float32))
    return pl.pallas_call(
        functools.partial(column_kernel, final),
        in_specs=[smem] + [vmem] * 7,
        out_specs=[vmem] * len(out_shape),
        out_shape=out_shape,
        scratch_shapes=[
            pltpu.VMEM(peaks.shape, jnp.float32),
            pltpu.VMEM((2 * matrix.shape[1], rows, 128), jnp.float32),
        ],
        compiler_params=pltpu.CompilerParams(vmem_limit_bytes=8 * MIB),
        name="columns",
    )(table, level, *parts, matrix, peaks)


def row_kernel(table, level, sums, matrix, peaks, out, weights, gathered, spread):
    blocks, block_rows = out.shape
    listed, rows = matrix.shape[1:3]
    for e in range(2 * listed):
        gathered[e : e + 1, :] = sums[pl.ds(table[SLOTS + e], 1), :]
    factors = (1.0 / (1.0 + gathered[...])).T
    for e in range(2 * listed):
        spread[e] = jnp.broadcast_to(factors[:, e : e + 1], (rows, 128))
    for s in range(blocks):
        weights[s] = jnp.exp2(peaks[s] - level[s : s + 1, :])
    lanes = block_rows // 128
    for s in range(blocks):
        g = s // SHARE

        def one_entry(t, total):
            k = table[ORDER + s * listed + t]
            acc = [jnp.zeros((8, 128), jnp.float32) for _ in range(lanes)]
            for j in range(0, rows, 8):
                v = spread[g * listed + k, j : j + 8, :]
                for l in range(lanes):
                    acc[l] = acc[l] + matrix[s, k, j : j + 8, 128 * l : 128 * l + 128] * v
            w = weights[s, pl.ds(k, 1), :]
            return tuple(t + a * w[:, 128 * l : 128 * l + 128] for l, (t, a) in enumerate(zip(total, acc)))

        total = lax.fori_loop(
            0, table[COUNTS + s], one_entry, tuple(jnp.zeros((8, 128), jnp.float32) for _ in range(lanes))
        )
        out[s : s + 1, :] = jnp.concatenate([jnp.sum(t, axis=0, keepdims=True) for t in total], axis=1)


def row_pass(table, level, sums, matrix, peaks):
    blocks, block_rows = level.shape
    listed, rows = matrix.shape[1:3]
    vmem = pl.BlockSpec(memory_space=pltpu.VMEM)
    smem = pl.BlockSpec(memory_space=pltpu.SMEM)
    return pl.pallas_call(
        row_kernel,
        in_specs=[smem] + [vmem] * 4,
        out_specs=vmem,
        out_shape=jax.ShapeDtypeStruct((blocks, block_rows), jnp.float32),
        scratch_shapes=[
            pltpu.VMEM(peaks.shape, jnp.float32),
            pltpu.VMEM((128, rows), jnp.float32),
            pltpu.VMEM((2 * listed, rows, 128), jnp.float32),
        ],
        compiler_params=pltpu.CompilerParams(vmem_limit_bytes=8 * MIB),
        name="rows",
    )(table, level, sums, matrix, peaks)


def from_columns(x):
    return [x] + [lax.ppermute(x, "col", [(i, (i + d) % 4) for i in range(4)]) for d in (1, 2, 3)]


def sum_over_rows(x):
    x = x + send(x, 0, 0, 1)
    x = x + send(x, 0, 1, 0) + send(x, 0, 2, 0) + send(x, 0, 3, 0)
    return x + send(x, 1, 0, 0) + send(x, 2, 0, 0) + send(x, 3, 0, 0)


def tables_kernel(target_blocks, me, pairs, counts, owners, source, table, loaded, listing, sems):
    blocks, listed = pairs.shape
    copies = [pltpu.make_async_copy(source.at[s], loaded.at[s], sems.at[s]) for s in range(blocks)]
    for copy in copies:
        copy.start()
    starts = np.cumsum([0] + [len(stage) for stage in piece_layout()])
    z, y, core = me[0] // 8, (me[0] // 2) % 4, me[0] % 2
    for n in range(int(starts[-1])):
        table[DEST + n] = -1
    for g in range(blocks // SHARE):
        found = []
        for k in range(listed):
            slot = owners[pairs[g * SHARE, k]]
            owner, which = slot // target_blocks, slot % target_blocks
            dz = (owner // 8 - z + 4) % 4
            dy = ((owner // 2) % 4 - y + 4) % 4
            other = jnp.where(owner % 2 == core, 0, 1)
            across = jnp.where(which == 0, dz, dy)
            along = jnp.where(which == 0, dy, dz)
            stage = jnp.where(across == 0, 0, jnp.where(across == 2, 2, 1))
            index = jnp.where(along == 0, 0, jnp.where(along == 3, 1, along + 1))
            set_at = other * 2 + which
            near = 2 * set_at + jnp.where(across == 3, 0, 1)
            position = index + 4 * jnp.where(stage == 1, near, set_at)
            base = jnp.where(stage == 0, int(starts[0]), jnp.where(stage == 1, int(starts[1]), int(starts[2])))
            found.append((slot, stage, base + position))
        following = []
        begin = jnp.int32(0)
        for stage in range(STAGES):
            table[SEGMENTS + g * (STAGES + 1) + stage] = begin
            following.append(begin)
            begin = begin + sum(jnp.where(f[1] == stage, 1, 0) for f in found)
        table[SEGMENTS + g * (STAGES + 1) + STAGES] = begin
        for k, (slot, stage, position) in enumerate(found):
            place = jnp.where(stage == 0, following[0], jnp.where(stage == 1, following[1], following[2]))
            following = [f + jnp.where(stage == n, 1, 0) for n, f in enumerate(following)]
            table[SLOTS + g * listed + place] = slot
            table[DEST + position] = g * listed + place
            listing[place] = k
        for s in range(g * SHARE, (g + 1) * SHARE):
            count = counts[s]
            table[COUNTS + s] = count
            for stage in range(STAGES):
                table[LIVES + s * STAGES + stage] = sum(
                    jnp.where((f[1] == stage) & (k < count), 1, 0) for k, f in enumerate(found)
                )
            turn = jnp.int32(0)
            for place in range(listed):
                live = jnp.where(listing[place] < count, 1, 0)
                table[ORDER + s * listed + turn] = place
                table[ALIVE + s * listed + place] = live
                turn = turn + live
    for copy in copies:
        copy.wait()


def tables(pair_list, counts, owner_map, source_vectors, target_blocks):
    listed = pair_list.shape[1]
    me = jnp.reshape(lax.axis_index("row"), (1,)).astype(jnp.int32)
    smem = pl.BlockSpec(memory_space=pltpu.SMEM)
    return pl.pallas_call(
        functools.partial(tables_kernel, target_blocks),
        in_specs=[smem] * 4 + [pl.BlockSpec(memory_space=pltpu.HBM)],
        out_specs=[smem, pl.BlockSpec(memory_space=pltpu.VMEM)],
        out_shape=[
            jax.ShapeDtypeStruct((TABLE,), jnp.int32),
            pltpu.VMEM(source_vectors.shape, source_vectors.dtype),
        ],
        scratch_shapes=[pltpu.SMEM((listed,), jnp.int32), pltpu.SemaphoreType.DMA(source_vectors.shape[:1])],
        compiler_params=pltpu.CompilerParams(vmem_limit_bytes=4 * MIB),
        name="tables",
    )(me, pair_list, counts, owner_map, source_vectors)


def shards(source_vectors, target_vectors, pair_list, counts, owner_map):
    target_blocks, quarter, _ = target_vectors.shape
    listed = pair_list.shape[1]
    targets = owner_map.shape[0]
    source_vectors = pltpu.with_memory_space_constraint(source_vectors, pltpu.HBM)
    table, loaded = tables(pair_list, counts, owner_map, source_vectors, target_blocks)

    def stage(number, pieces, earlier):
        pieces = pieces + [send(piece, 0, 0, 1) for piece in pieces]
        pieces = [pltpu.with_memory_space_constraint(piece, pltpu.HBM) for piece in pieces]
        return score_stage(number, listed, table, loaded, pieces, earlier)

    along_y, along_z = target_vectors[:1], target_vectors[1:]
    arrived = ring_sends(along_y, 0, 1) + ring_sends(along_z, 1, 0)
    *arrived, table, loaded = tie(*arrived, table, loaded)
    loaded = pltpu.with_memory_space_constraint(loaded, pltpu.VMEM)
    first = [jnp.concatenate([along_y] + arrived[:3], axis=0), jnp.concatenate([along_z] + arrived[3:], axis=0)]
    second = [
        send(first[0], 1, 0, 0),
        send(first[0], -1, 0, 0),
        send(first[1], 0, 1, 0),
        send(first[1], 0, -1, 0),
    ]
    done = stage(0, first, [])
    *second, peaks = tie(*second, done[1])
    third = [
        send(second[0][:2], 1, 0, 0),
        send(second[1][2:], -1, 0, 0),
        send(second[2][:2], 0, 1, 0),
        send(second[3][2:], 0, -1, 0),
    ]
    done = stage(1, second, [done[0], peaks, done[2]])
    *third, peaks = tie(*third, done[1])
    matrix, peaks, _, high, total = stage(2, third, [done[0], peaks, done[2]])
    matrix = pltpu.with_memory_space_constraint(matrix, pltpu.VMEM)

    both = from_columns(jnp.stack([high, total]))
    level = jnp.maximum(functools.reduce(jnp.maximum, [b[0] for b in both]), 0.0)
    parts = [b[1] * jnp.exp2(b[0] - level) for b in both]

    for sweep_index in range(SWEEPS):
        final = sweep_index == SWEEPS - 1
        sums = column_pass(final, table, targets, level, parts, matrix, peaks)
        if final:
            break
        sums = sum_over_rows(sums[0])
        parts = from_columns(row_pass(table, level, sums, matrix, peaks))
    sums, source_dual = sums
    row_count = targets // target_blocks
    back = lax.all_to_all(
        sums.reshape(row_count, target_blocks, quarter), "row", split_axis=0, concat_axis=0, tiled=True
    )
    target_dual = -EPSILON * jnp.log(1.0 + jnp.sum(back, axis=0))
    return source_dual, target_dual


def solution(mesh):
    return jax.shard_map(
        shards,
        mesh=mesh,
        in_specs=(P("row", None, None), P("row", "col", None), P("row", None), P("row"), P()),
        out_specs=(P("row", None), P("row", "col")),
        check_vma=False,
    )
```

```python
import functools

import jax
import jax.numpy as jnp
import numpy as np
from jax import lax
from jax.experimental import pallas as pl
from jax.experimental.pallas import tpu as pltpu
from jax.sharding import PartitionSpec as P

SHARE = 4
SWEEPS = 3
EPSILON = 0.05
LOG2E = 1.4426950408889634
LN2 = 0.6931471805599453
SCALE = LOG2E / EPSILON
NEGATIVE = -1e30
MIB = 2**20


def row_perm(dz, dy, dc):
    return [
        ((z * 4 + y) * 2 + c, (((z + dz) % 4) * 4 + (y + dy) % 4) * 2 + (c ^ dc))
        for z in range(4)
        for y in range(4)
        for c in range(2)
    ]


def send(x, dz, dy, dc):
    return lax.ppermute(x, "row", row_perm(dz, dy, dc))


RING = (0, -1, 1, 2)
STAGES = 3
TOGETHER = (1, 2, 4)


def tie(*arrays):
    return lax.optimization_barrier(arrays)


def ring_sends(own, dz, dy):
    return [send(own, dz, dy, 0), send(own, -dz, -dy, 0), send(own, 2 * dz, 2 * dy, 0)]


def piece_layout():
    first = [(core, which, 0, RING) for core in range(2) for which in range(2)]
    second = [(core, which, d, RING) for core in range(2) for which in range(2) for d in (-1, 1)]
    third = [
        (core, which, 2, half) for core in range(2) for which in range(2) for half in (RING[:2], RING[2:])
    ]
    stages = []
    for pieces in (first, second, third):
        entries = []
        for piece, (core, which, across, ring) in enumerate(pieces):
            for index, along in enumerate(ring):
                dz, dy = (across, along) if which == 0 else (along, across)
                entries.append((piece, index, dz, dy, core, which))
        stages.append(entries)
    return stages


SLOTS, DEST, SEGMENTS, LIVES, ORDER, USERS, COUNTS, USES, TABLE = 0, 24, 88, 96, 120, 216, 312, 320, 344


def score_kernel(stage, listed, table, source, *refs):
    layout = piece_layout()[stage]
    number = max(entry[0] for entry in layout) + 1
    pieces, refs = refs[:number], refs[number:]
    if stage > 0:
        refs = refs[3:]
    matrix, peak_out, sum_out = refs[:3]
    if stage == STAGES - 1:
        high_out, total_out = refs[3:5]
    held, fetch_sems = refs[-2:]
    blocks = source.shape[0]
    rows = matrix.shape[2]

    def stream(s):
        return pltpu.make_async_copy(source.at[s], streamed.at[lax.rem(s, 2)], stream_sems.at[lax.rem(s, 2)])


    def fetch(piece, index, entry):
        return pltpu.make_async_copy(
            pieces[piece].at[index], held.at[pl.ds(entry * rows, rows)], fetch_sems.at[entry]
        )

    offset = DEST + sum(len(entries) for entries in piece_layout()[:stage])
    for position, (piece, index, *_) in enumerate(layout, offset):

        @pl.when(table[position] >= 0)
        def _():
            fetch(piece, index, table[position]).start()

    if stage == 0:
        peak_out[...] = jnp.full(peak_out.shape, NEGATIVE, jnp.float32)
        sum_out[...] = jnp.zeros(sum_out.shape, jnp.float32)

    together = TOGETHER[stage]
    largest = 8 // together if together > 1 else 4

    def some_blocks(turn, carry):
        group = turn * together // SHARE
        begin = table[SEGMENTS + group * (STAGES + 1) + stage]
        alive = [table[LIVES + (turn * together + m) * STAGES + stage] for m in range(together)]
        live = functools.reduce(jnp.maximum, alive)

        @pl.when(lax.rem(turn * together, SHARE) == 0)
        def _():
            def arrive(entry, carry):
                fetch(0, 0, group * listed + entry).wait()
                return carry

            lax.fori_loop(begin, table[SEGMENTS + group * (STAGES + 1) + stage + 1], arrive, 0)

        def batch(first, size):
            base = pl.multiple_of((group * listed + begin + first) * rows, rows)
            vectors = held[pl.ds(base, size * rows), :]
            scores = [
                lax.dot_general(
                    vectors,
                    source[turn * together + m],
                    (((1,), (1,)), ((), ())),
                    preferred_element_type=jnp.float32,
                )
                for m in range(together)
            ]
            for m in range(together):
                s = turn * together + m
                for p in range(size):
                    one = scores[m][p * rows : (p + 1) * rows] * SCALE
                    peak = jnp.max(one, axis=0, keepdims=True)
                    lifted = jnp.exp2(one - peak)
                    matrix[s, begin + first + p] = lifted
                    total = jnp.sum(lifted, axis=0, keepdims=True)
                    if together > 1:
                        used = first + p < alive[m]
                        peak, total = jnp.where(used, peak, NEGATIVE), jnp.where(used, total, 0.0)
                    peak_out[s, pl.ds(begin + first + p, 1), :] = peak
                    sum_out[s, pl.ds(begin + first + p, 1), :] = total

        def whole(q, carry):
            batch(largest * q, largest)
            return carry

        lax.fori_loop(0, live // largest, whole, 0)
        for size in range(1, largest):
            pl.when(lax.rem(live, largest) == size)(functools.partial(batch, live - size, size))
        return carry

    lax.fori_loop(0, blocks // together, some_blocks, 0)
    if stage == STAGES - 1:
        for s in range(blocks):
            high = jnp.max(peak_out[s], axis=0, keepdims=True)
            high_out[s : s + 1, :] = high
            total_out[s : s + 1, :] = jnp.sum(sum_out[s] * jnp.exp2(peak_out[s] - high), axis=0, keepdims=True)


def score_stage(stage, listed, table, source_vectors, pieces, earlier):
    blocks, block_rows, width = source_vectors.shape
    rows = pieces[0].shape[1]
    padded = 16
    hbm = pl.BlockSpec(memory_space=pltpu.HBM)
    vmem = pl.BlockSpec(memory_space=pltpu.VMEM)
    smem = pl.BlockSpec(memory_space=pltpu.SMEM)
    last = stage == STAGES - 1
    share = (0.25, 0.5, 0.25)[stage]
    small = jax.ShapeDtypeStruct((blocks, padded, block_rows), jnp.float32)
    whole = jax.ShapeDtypeStruct((blocks, block_rows), jnp.float32)
    if earlier:
        earlier = [pltpu.with_memory_space_constraint(earlier[0], pltpu.VMEM)] + earlier[1:]
    return pl.pallas_call(
        functools.partial(score_kernel, stage, listed),
        in_specs=[smem, vmem] + [hbm] * len(pieces) + [vmem] * len(earlier),
        out_specs=[vmem] * (3 + 2 * last),
        out_shape=[pltpu.VMEM((blocks, listed, rows, block_rows), jnp.float32), small, small] + [whole] * 2 * last,
        scratch_shapes=[
            pltpu.VMEM((2 * listed * rows, width), jnp.bfloat16),
            pltpu.SemaphoreType.DMA((2 * listed,)),
        ],
        input_output_aliases={2 + len(pieces) + n: n for n in range(len(earlier))},
        compiler_params=pltpu.CompilerParams(vmem_limit_bytes=8 * MIB),
        cost_estimate=pl.CostEstimate(
            flops=int(2 * blocks * listed * rows * block_rows * width * share),
            bytes_accessed=int(4 * blocks * listed * rows * block_rows * share),
            transcendentals=0,
        ),
        name="scores",
    )(table, source_vectors, *pieces, *earlier)


def column_kernel(final, table, level, part, near, far, back, matrix, peaks, *refs):
    sums_out = refs[0]
    weights, columns = refs[-2:]
    blocks, block_rows = part.shape
    listed, rows = matrix.shape[1:3]
    total = part[...] + near[...] + far[...] + back[...] + jnp.exp2(-level[...])
    inverse = 1.0 / total
    if final:
        refs[1][...] = -EPSILON * LN2 * (level[...] + jnp.log2(total))
    for s in range(blocks):
        weights[s] = jnp.exp2(peaks[s] - level[s : s + 1, :]) * inverse[s : s + 1, :]
    sums_out[...] = jnp.zeros_like(sums_out)
    lanes = block_rows // 128

    for g in range(blocks // SHARE):

        def one_entry(k, carry):
            entry = g * listed + k

            def one_source(t, acc):
                s = table[USERS + entry * SHARE + t]
                w = weights[s, pl.ds(k, 1), :]
                spread = [jnp.broadcast_to(w[:, 128 * l : 128 * l + 128], (8, 128)) for l in range(lanes)]
                out = []
                for j, a in enumerate(acc):
                    parts = [
                        matrix[s, k, 8 * j : 8 * j + 8, 128 * l : 128 * l + 128] * spread[l] for l in range(lanes)
                    ]
                    out.append(a + (sum(parts[: lanes // 2]) + sum(parts[lanes // 2 :])))
                return tuple(out)

            acc = tuple(jnp.zeros((8, 128), jnp.float32) for _ in range(rows // 8))
            acc = lax.fori_loop(0, table[USES + entry], one_source, acc)
            for j, a in enumerate(acc):
                columns[g * listed + k, 8 * j : 8 * j + 8, :] = a
            return carry

        lax.fori_loop(0, listed, one_entry, 0)

    lane = lax.broadcasted_iota(jnp.int32, (8, 128), 1)
    merged = [jnp.zeros((8, 128), jnp.float32)] * (rows // 8)
    for e in range(2 * listed):
        for j in range(rows // 8):
            one = jnp.sum(columns[e, 8 * j : 8 * j + 8, :], axis=1, keepdims=True)
            merged[j] = jnp.where(lane == e, one, merged[j])
    by_entry = jnp.concatenate(merged, axis=0).T
    for e in range(2 * listed):
        sums_out[pl.ds(table[SLOTS + e], 1), :] = by_entry[e : e + 1, :]


def column_pass(final, table, targets, level, parts, matrix, peaks):
    blocks, block_rows = level.shape
    rows = matrix.shape[2]
    vmem = pl.BlockSpec(memory_space=pltpu.VMEM)
    smem = pl.BlockSpec(memory_space=pltpu.SMEM)
    out_shape = [jax.ShapeDtypeStruct((targets, rows), jnp.float32)]
    if final:
        out_shape.append(jax.ShapeDtypeStruct((blocks, block_rows), jnp.float32))
    return pl.pallas_call(
        functools.partial(column_kernel, final),
        in_specs=[smem] + [vmem] * 7,
        out_specs=[vmem] * len(out_shape),
        out_shape=out_shape,
        scratch_shapes=[
            pltpu.VMEM(peaks.shape, jnp.float32),
            pltpu.VMEM((2 * matrix.shape[1], rows, 128), jnp.float32),
        ],
        compiler_params=pltpu.CompilerParams(vmem_limit_bytes=8 * MIB),
        name="columns",
    )(table, level, *parts, matrix, peaks)


def row_kernel(table, level, sums, matrix, peaks, out, weights, gathered, spread):
    blocks, block_rows = out.shape
    listed, rows = matrix.shape[1:3]
    for e in range(2 * listed):
        gathered[e : e + 1, :] = sums[pl.ds(table[SLOTS + e], 1), :]
    factors = (1.0 / (1.0 + gathered[...])).T
    for e in range(2 * listed):
        spread[e] = jnp.broadcast_to(factors[:, e : e + 1], (rows, 128))
    for s in range(blocks):
        weights[s] = jnp.exp2(peaks[s] - level[s : s + 1, :])
    lanes = block_rows // 128
    for s in range(blocks):
        g = s // SHARE

        def one_entry(t, total):
            k = table[ORDER + s * listed + t]
            acc = [jnp.zeros((8, 128), jnp.float32) for _ in range(lanes)]
            for j in range(0, rows, 8):
                v = spread[g * listed + k, j : j + 8, :]
                for l in range(lanes):
                    acc[l] = acc[l] + matrix[s, k, j : j + 8, 128 * l : 128 * l + 128] * v
            w = weights[s, pl.ds(k, 1), :]
            return tuple(t + a * w[:, 128 * l : 128 * l + 128] for l, (t, a) in enumerate(zip(total, acc)))

        total = lax.fori_loop(
            0, table[COUNTS + s], one_entry, tuple(jnp.zeros((8, 128), jnp.float32) for _ in range(lanes))
        )
        out[s : s + 1, :] = jnp.concatenate([jnp.sum(t, axis=0, keepdims=True) for t in total], axis=1)


def row_pass(table, level, sums, matrix, peaks):
    blocks, block_rows = level.shape
    listed, rows = matrix.shape[1:3]
    vmem = pl.BlockSpec(memory_space=pltpu.VMEM)
    smem = pl.BlockSpec(memory_space=pltpu.SMEM)
    return pl.pallas_call(
        row_kernel,
        in_specs=[smem] + [vmem] * 4,
        out_specs=vmem,
        out_shape=jax.ShapeDtypeStruct((blocks, block_rows), jnp.float32),
        scratch_shapes=[
            pltpu.VMEM(peaks.shape, jnp.float32),
            pltpu.VMEM((128, rows), jnp.float32),
            pltpu.VMEM((2 * listed, rows, 128), jnp.float32),
        ],
        compiler_params=pltpu.CompilerParams(vmem_limit_bytes=8 * MIB),
        name="rows",
    )(table, level, sums, matrix, peaks)


def from_columns(x):
    return [x] + [lax.ppermute(x, "col", [(i, (i + d) % 4) for i in range(4)]) for d in (1, 2, 3)]


def sum_over_rows(x):
    x = x + send(x, 0, 0, 1)
    x = x + send(x, 0, 1, 0) + send(x, 0, 2, 0) + send(x, 0, 3, 0)
    return x + send(x, 1, 0, 0) + send(x, 2, 0, 0) + send(x, 3, 0, 0)


def tables_kernel(target_blocks, me, pairs, counts, owners, source, table, loaded, listing, sems):
    blocks, listed = pairs.shape
    copies = [pltpu.make_async_copy(source.at[s], loaded.at[s], sems.at[s]) for s in range(blocks)]
    for copy in copies:
        copy.start()
    starts = np.cumsum([0] + [len(stage) for stage in piece_layout()])
    z, y, core = me[0] // 8, (me[0] // 2) % 4, me[0] % 2
    for n in range(int(starts[-1])):
        table[DEST + n] = -1
    for g in range(blocks // SHARE):
        found = []
        for k in range(listed):
            slot = owners[pairs[g * SHARE, k]]
            owner, which = slot // target_blocks, slot % target_blocks
            dz = (owner // 8 - z + 4) % 4
            dy = ((owner // 2) % 4 - y + 4) % 4
            other = jnp.where(owner % 2 == core, 0, 1)
            across = jnp.where(which == 0, dz, dy)
            along = jnp.where(which == 0, dy, dz)
            stage = jnp.where(across == 0, 0, jnp.where(across == 2, 2, 1))
            index = jnp.where(along == 0, 0, jnp.where(along == 3, 1, along + 1))
            set_at = other * 2 + which
            near = 2 * set_at + jnp.where(across == 3, 0, 1)
            position = index + 4 * jnp.where(stage == 1, near, set_at)
            base = jnp.where(stage == 0, int(starts[0]), jnp.where(stage == 1, int(starts[1]), int(starts[2])))
            found.append((slot, stage, base + position))
        following = []
        begin = jnp.int32(0)
        for stage in range(STAGES):
            table[SEGMENTS + g * (STAGES + 1) + stage] = begin
            following.append(begin)
            begin = begin + sum(jnp.where(f[1] == stage, 1, 0) for f in found)
        table[SEGMENTS + g * (STAGES + 1) + STAGES] = begin
        for k, (slot, stage, position) in enumerate(found):
            place = jnp.where(stage == 0, following[0], jnp.where(stage == 1, following[1], following[2]))
            following = [f + jnp.where(stage == n, 1, 0) for n, f in enumerate(following)]
            table[SLOTS + g * listed + place] = slot
            table[DEST + position] = g * listed + place
            listing[place] = k
        for s in range(g * SHARE, (g + 1) * SHARE):
            count = counts[s]
            table[COUNTS + s] = count
            for stage in range(STAGES):
                table[LIVES + s * STAGES + stage] = sum(
                    jnp.where((f[1] == stage) & (k < count), 1, 0) for k, f in enumerate(found)
                )
            turn = jnp.int32(0)
            for place in range(listed):
                live = jnp.where(listing[place] < count, 1, 0)
                table[ORDER + s * listed + turn] = place
                turn = turn + live
        for place in range(listed):
            entry = g * listed + place
            used = jnp.int32(0)
            for s in range(g * SHARE, (g + 1) * SHARE):
                table[USERS + entry * SHARE + used] = s
                used = used + jnp.where(listing[place] < counts[s], 1, 0)
            table[USES + entry] = used
    for copy in copies:
        copy.wait()


def tables(pair_list, counts, owner_map, source_vectors, target_blocks):
    listed = pair_list.shape[1]
    me = jnp.reshape(lax.axis_index("row"), (1,)).astype(jnp.int32)
    smem = pl.BlockSpec(memory_space=pltpu.SMEM)
    return pl.pallas_call(
        functools.partial(tables_kernel, target_blocks),
        in_specs=[smem] * 4 + [pl.BlockSpec(memory_space=pltpu.HBM)],
        out_specs=[smem, pl.BlockSpec(memory_space=pltpu.VMEM)],
        out_shape=[
            jax.ShapeDtypeStruct((TABLE,), jnp.int32),
            pltpu.VMEM(source_vectors.shape, source_vectors.dtype),
        ],
        scratch_shapes=[pltpu.SMEM((listed,), jnp.int32), pltpu.SemaphoreType.DMA(source_vectors.shape[:1])],
        compiler_params=pltpu.CompilerParams(vmem_limit_bytes=4 * MIB),
        name="tables",
    )(me, pair_list, counts, owner_map, source_vectors)


def shards(source_vectors, target_vectors, pair_list, counts, owner_map):
    target_blocks, quarter, _ = target_vectors.shape
    listed = pair_list.shape[1]
    targets = owner_map.shape[0]
    source_vectors = pltpu.with_memory_space_constraint(source_vectors, pltpu.HBM)
    table, loaded = tables(pair_list, counts, owner_map, source_vectors, target_blocks)

    def stage(number, pieces, earlier):
        pieces = pieces + [send(piece, 0, 0, 1) for piece in pieces]
        pieces = [pltpu.with_memory_space_constraint(piece, pltpu.HBM) for piece in pieces]
        return score_stage(number, listed, table, loaded, pieces, earlier)

    along_y, along_z = target_vectors[:1], target_vectors[1:]
    arrived = ring_sends(along_y, 0, 1) + ring_sends(along_z, 1, 0)
    *arrived, table, loaded = tie(*arrived, table, loaded)
    loaded = pltpu.with_memory_space_constraint(loaded, pltpu.VMEM)
    first = [jnp.concatenate([along_y] + arrived[:3], axis=0), jnp.concatenate([along_z] + arrived[3:], axis=0)]
    second = [
        send(first[0], 1, 0, 0),
        send(first[0], -1, 0, 0),
        send(first[1], 0, 1, 0),
        send(first[1], 0, -1, 0),
    ]
    done = stage(0, first, [])
    *second, peaks = tie(*second, done[1])
    third = [
        send(second[0][:2], 1, 0, 0),
        send(second[1][2:], -1, 0, 0),
        send(second[2][:2], 0, 1, 0),
        send(second[3][2:], 0, -1, 0),
    ]
    done = stage(1, second, [done[0], peaks, done[2]])
    *third, peaks = tie(*third, done[1])
    matrix, peaks, _, high, total = stage(2, third, [done[0], peaks, done[2]])
    matrix = pltpu.with_memory_space_constraint(matrix, pltpu.VMEM)

    both = from_columns(jnp.stack([high, total]))
    level = jnp.maximum(functools.reduce(jnp.maximum, [b[0] for b in both]), 0.0)
    parts = [b[1] * jnp.exp2(b[0] - level) for b in both]

    for sweep_index in range(SWEEPS):
        final = sweep_index == SWEEPS - 1
        sums = column_pass(final, table, targets, level, parts, matrix, peaks)
        if final:
            break
        sums = sum_over_rows(sums[0])
        parts = from_columns(row_pass(table, level, sums, matrix, peaks))
    sums, source_dual = sums
    row_count = targets // target_blocks
    back = lax.all_to_all(
        sums.reshape(row_count, target_blocks, quarter), "row", split_axis=0, concat_axis=0, tiled=True
    )
    target_dual = -EPSILON * jnp.log(1.0 + jnp.sum(back, axis=0))
    return source_dual, target_dual


def solution(mesh):
    return jax.shard_map(
        shards,
        mesh=mesh,
        in_specs=(P("row", None, None), P("row", "col", None), P("row", None), P("row"), P()),
        out_specs=(P("row", None), P("row", "col")),
        check_vma=False,
    )
```

```python
import functools

import jax
import jax.numpy as jnp
import numpy as np
from jax import lax
from jax.experimental import pallas as pl
from jax.experimental.pallas import tpu as pltpu
from jax.sharding import PartitionSpec as P

SHARE = 4
SWEEPS = 3
EPSILON = 0.05
LOG2E = 1.4426950408889634
LN2 = 0.6931471805599453
SCALE = LOG2E / EPSILON
NEGATIVE = -1e30
MIB = 2**20


def row_perm(dz, dy, dc):
    return [
        ((z * 4 + y) * 2 + c, (((z + dz) % 4) * 4 + (y + dy) % 4) * 2 + (c ^ dc))
        for z in range(4)
        for y in range(4)
        for c in range(2)
    ]


def send(x, dz, dy, dc):
    return lax.ppermute(x, "row", row_perm(dz, dy, dc))


RING = (0, -1, 1, 2)
STAGES = 3
TOGETHER = (1, 2, 4)


def tie(*arrays):
    return lax.optimization_barrier(arrays)


def ring_sends(own, dz, dy):
    return [send(own, dz, dy, 0), send(own, -dz, -dy, 0), send(own, 2 * dz, 2 * dy, 0)]


def piece_layout():
    first = [(core, which, 0, RING) for core in range(2) for which in range(2)]
    second = [(core, which, d, RING) for core in range(2) for which in range(2) for d in (-1, 1)]
    third = [
        (core, which, 2, half) for core in range(2) for which in range(2) for half in (RING[:2], RING[2:])
    ]
    stages = []
    for pieces in (first, second, third):
        entries = []
        for piece, (core, which, across, ring) in enumerate(pieces):
            for index, along in enumerate(ring):
                dz, dy = (across, along) if which == 0 else (along, across)
                entries.append((piece, index, dz, dy, core, which))
        stages.append(entries)
    return stages


SLOTS, DEST, SEGMENTS, LIVES, ORDER, ALIVE, COUNTS, TABLE = 0, 24, 88, 96, 120, 216, 312, 320


def score_kernel(stage, listed, table, source, *refs):
    layout = piece_layout()[stage]
    number = max(entry[0] for entry in layout) + 1
    pieces, refs = refs[:number], refs[number:]
    if stage > 0:
        refs = refs[3:]
    matrix, peak_out, sum_out = refs[:3]
    if stage == STAGES - 1:
        high_out, total_out = refs[3:5]
    held, fetch_sems = refs[-2:]
    blocks = source.shape[0]
    rows = matrix.shape[2]

    def stream(s):
        return pltpu.make_async_copy(source.at[s], streamed.at[lax.rem(s, 2)], stream_sems.at[lax.rem(s, 2)])


    def fetch(piece, index, entry):
        return pltpu.make_async_copy(
            pieces[piece].at[index], held.at[pl.ds(entry * rows, rows)], fetch_sems.at[entry]
        )

    offset = DEST + sum(len(entries) for entries in piece_layout()[:stage])
    for position, (piece, index, *_) in enumerate(layout, offset):

        @pl.when(table[position] >= 0)
        def _():
            fetch(piece, index, table[position]).start()

    if stage == 0:
        peak_out[...] = jnp.full(peak_out.shape, NEGATIVE, jnp.float32)
        sum_out[...] = jnp.zeros(sum_out.shape, jnp.float32)

    together = TOGETHER[stage]
    largest = 8 // together if together > 1 else 4

    def some_blocks(turn, carry):
        group = turn * together // SHARE
        begin = table[SEGMENTS + group * (STAGES + 1) + stage]
        alive = [table[LIVES + (turn * together + m) * STAGES + stage] for m in range(together)]
        live = functools.reduce(jnp.maximum, alive)

        @pl.when(lax.rem(turn * together, SHARE) == 0)
        def _():
            def arrive(entry, carry):
                fetch(0, 0, group * listed + entry).wait()
                return carry

            lax.fori_loop(begin, table[SEGMENTS + group * (STAGES + 1) + stage + 1], arrive, 0)

        def batch(first, size):
            base = pl.multiple_of((group * listed + begin + first) * rows, rows)
            vectors = held[pl.ds(base, size * rows), :]
            scores = [
                lax.dot_general(
                    vectors,
                    source[turn * together + m],
                    (((1,), (1,)), ((), ())),
                    preferred_element_type=jnp.float32,
                )
                for m in range(together)
            ]
            for m in range(together):
                s = turn * together + m
                for p in range(size):
                    one = scores[m][p * rows : (p + 1) * rows] * SCALE
                    peak = jnp.max(one, axis=0, keepdims=True)
                    lifted = jnp.exp2(one - peak)
                    matrix[s, begin + first + p] = lifted
                    total = jnp.sum(lifted, axis=0, keepdims=True)
                    if together > 1:
                        used = first + p < alive[m]
                        peak, total = jnp.where(used, peak, NEGATIVE), jnp.where(used, total, 0.0)
                    peak_out[s, pl.ds(begin + first + p, 1), :] = peak
                    sum_out[s, pl.ds(begin + first + p, 1), :] = total

        def whole(q, carry):
            batch(largest * q, largest)
            return carry

        lax.fori_loop(0, live // largest, whole, 0)
        for size in range(1, largest):
            pl.when(lax.rem(live, largest) == size)(functools.partial(batch, live - size, size))
        return carry

    lax.fori_loop(0, blocks // together, some_blocks, 0)
    if stage == STAGES - 1:
        for s in range(blocks):
            high = jnp.max(peak_out[s], axis=0, keepdims=True)
            high_out[s : s + 1, :] = high
            total_out[s : s + 1, :] = jnp.sum(sum_out[s] * jnp.exp2(peak_out[s] - high), axis=0, keepdims=True)


def score_stage(stage, listed, table, source_vectors, pieces, earlier):
    blocks, block_rows, width = source_vectors.shape
    rows = pieces[0].shape[1]
    padded = 16
    hbm = pl.BlockSpec(memory_space=pltpu.HBM)
    vmem = pl.BlockSpec(memory_space=pltpu.VMEM)
    smem = pl.BlockSpec(memory_space=pltpu.SMEM)
    last = stage == STAGES - 1
    share = (0.25, 0.5, 0.25)[stage]
    small = jax.ShapeDtypeStruct((blocks, padded, block_rows), jnp.float32)
    whole = jax.ShapeDtypeStruct((blocks, block_rows), jnp.float32)
    if earlier:
        earlier = [pltpu.with_memory_space_constraint(earlier[0], pltpu.VMEM)] + earlier[1:]
    return pl.pallas_call(
        functools.partial(score_kernel, stage, listed),
        in_specs=[smem, vmem] + [hbm] * len(pieces) + [vmem] * len(earlier),
        out_specs=[vmem] * (3 + 2 * last),
        out_shape=[pltpu.VMEM((blocks, listed, rows, block_rows), jnp.float32), small, small] + [whole] * 2 * last,
        scratch_shapes=[
            pltpu.VMEM((2 * listed * rows, width), jnp.bfloat16),
            pltpu.SemaphoreType.DMA((2 * listed,)),
        ],
        input_output_aliases={2 + len(pieces) + n: n for n in range(len(earlier))},
        compiler_params=pltpu.CompilerParams(vmem_limit_bytes=8 * MIB),
        cost_estimate=pl.CostEstimate(
            flops=int(2 * blocks * listed * rows * block_rows * width * share),
            bytes_accessed=int(4 * blocks * listed * rows * block_rows * share),
            transcendentals=0,
        ),
        name="scores",
    )(table, source_vectors, *pieces, *earlier)


def column_kernel(final, table, level, part, near, far, back, matrix, peaks, *refs):
    sums_out = refs[0]
    weights, columns = refs[-2:]
    blocks, block_rows = part.shape
    listed, rows = matrix.shape[1:3]
    total = part[...] + near[...] + far[...] + back[...] + jnp.exp2(-level[...])
    inverse = 1.0 / total
    if final:
        refs[1][...] = -EPSILON * LN2 * (level[...] + jnp.log2(total))
    for s in range(blocks):
        weights[s] = jnp.exp2(peaks[s] - level[s : s + 1, :]) * inverse[s : s + 1, :]
    sums_out[...] = jnp.zeros_like(sums_out)
    lanes = block_rows // 128

    for g in range(blocks // SHARE):

        def one_entry(k, carry):
            def one_source(s, acc):
                w = weights[s, pl.ds(k, 1), :]
                spread = [jnp.broadcast_to(w[:, 128 * l : 128 * l + 128], (8, 128)) for l in range(lanes)]
                return tuple(
                    a + sum(matrix[s, k, 8 * j : 8 * j + 8, 128 * l : 128 * l + 128] * spread[l] for l in range(lanes))
                    for j, a in enumerate(acc)
                )

            acc = tuple(jnp.zeros((8, 128), jnp.float32) for _ in range(rows // 8))
            for s in range(g * SHARE, (g + 1) * SHARE):
                live = table[ALIVE + s * listed + k] > 0
                acc = lax.cond(live, functools.partial(one_source, s), lambda acc: acc, acc)
            for j, a in enumerate(acc):
                columns[g * listed + k, 8 * j : 8 * j + 8, :] = a
            return carry

        lax.fori_loop(0, listed, one_entry, 0)

    lane = lax.broadcasted_iota(jnp.int32, (8, 128), 1)
    merged = [jnp.zeros((8, 128), jnp.float32)] * (rows // 8)
    for e in range(2 * listed):
        for j in range(rows // 8):
            one = jnp.sum(columns[e, 8 * j : 8 * j + 8, :], axis=1, keepdims=True)
            merged[j] = jnp.where(lane == e, one, merged[j])
    by_entry = jnp.concatenate(merged, axis=0).T
    for e in range(2 * listed):
        sums_out[pl.ds(table[SLOTS + e], 1), :] = by_entry[e : e + 1, :]


def column_pass(final, table, targets, level, parts, matrix, peaks):
    blocks, block_rows = level.shape
    rows = matrix.shape[2]
    vmem = pl.BlockSpec(memory_space=pltpu.VMEM)
    smem = pl.BlockSpec(memory_space=pltpu.SMEM)
    out_shape = [jax.ShapeDtypeStruct((targets, rows), jnp.float32)]
    if final:
        out_shape.append(jax.ShapeDtypeStruct((blocks, block_rows), jnp.float32))
    return pl.pallas_call(
        functools.partial(column_kernel, final),
        in_specs=[smem] + [vmem] * 7,
        out_specs=[vmem] * len(out_shape),
        out_shape=out_shape,
        scratch_shapes=[
            pltpu.VMEM(peaks.shape, jnp.float32),
            pltpu.VMEM((2 * matrix.shape[1], rows, 128), jnp.float32),
        ],
        compiler_params=pltpu.CompilerParams(vmem_limit_bytes=8 * MIB),
        name="columns",
    )(table, level, *parts, matrix, peaks)


def row_kernel(table, level, sums, matrix, peaks, out, weights, gathered, spread):
    blocks, block_rows = out.shape
    listed, rows = matrix.shape[1:3]
    for e in range(2 * listed):
        gathered[e : e + 1, :] = sums[pl.ds(table[SLOTS + e], 1), :]
    factors = (1.0 / (1.0 + gathered[...])).T
    for e in range(2 * listed):
        spread[e] = jnp.broadcast_to(factors[:, e : e + 1], (rows, 128))
    for s in range(blocks):
        weights[s] = jnp.exp2(peaks[s] - level[s : s + 1, :])
    lanes = block_rows // 128
    for s in range(blocks):
        g = s // SHARE

        def one_entry(t, total):
            k = table[ORDER + s * listed + t]
            acc = [jnp.zeros((8, 128), jnp.float32) for _ in range(lanes)]
            for j in range(0, rows, 8):
                v = spread[g * listed + k, j : j + 8, :]
                for l in range(lanes):
                    acc[l] = acc[l] + matrix[s, k, j : j + 8, 128 * l : 128 * l + 128] * v
            w = weights[s, pl.ds(k, 1), :]
            return tuple(t + a * w[:, 128 * l : 128 * l + 128] for l, (t, a) in enumerate(zip(total, acc)))

        total = lax.fori_loop(
            0, table[COUNTS + s], one_entry, tuple(jnp.zeros((8, 128), jnp.float32) for _ in range(lanes))
        )
        out[s : s + 1, :] = jnp.concatenate([jnp.sum(t, axis=0, keepdims=True) for t in total], axis=1)


def row_pass(table, level, sums, matrix, peaks):
    blocks, block_rows = level.shape
    listed, rows = matrix.shape[1:3]
    vmem = pl.BlockSpec(memory_space=pltpu.VMEM)
    smem = pl.BlockSpec(memory_space=pltpu.SMEM)
    return pl.pallas_call(
        row_kernel,
        in_specs=[smem] + [vmem] * 4,
        out_specs=vmem,
        out_shape=jax.ShapeDtypeStruct((blocks, block_rows), jnp.float32),
        scratch_shapes=[
            pltpu.VMEM(peaks.shape, jnp.float32),
            pltpu.VMEM((128, rows), jnp.float32),
            pltpu.VMEM((2 * listed, rows, 128), jnp.float32),
        ],
        compiler_params=pltpu.CompilerParams(vmem_limit_bytes=8 * MIB),
        name="rows",
    )(table, level, sums, matrix, peaks)


def from_columns(x):
    return [x] + [lax.ppermute(x, "col", [(i, (i + d) % 4) for i in range(4)]) for d in (1, 2, 3)]


def sum_over_rows(x):
    x = x + send(x, 0, 0, 1)
    x = x + send(x, 0, 1, 0) + send(x, 0, 2, 0) + send(x, 0, 3, 0)
    return x + send(x, 1, 0, 0) + send(x, 2, 0, 0) + send(x, 3, 0, 0)


def tables_kernel(target_blocks, me, pairs, counts, owners, source, table, loaded, listing, sems):
    blocks, listed = pairs.shape
    copies = [pltpu.make_async_copy(source.at[s], loaded.at[s], sems.at[s]) for s in range(blocks)]
    for copy in copies:
        copy.start()
    starts = np.cumsum([0] + [len(stage) for stage in piece_layout()])
    z, y, core = me[0] // 8, (me[0] // 2) % 4, me[0] % 2
    for n in range(int(starts[-1])):
        table[DEST + n] = -1
    for g in range(blocks // SHARE):
        found = []
        for k in range(listed):
            slot = owners[pairs[g * SHARE, k]]
            owner, which = slot // target_blocks, slot % target_blocks
            dz = (owner // 8 - z + 4) % 4
            dy = ((owner // 2) % 4 - y + 4) % 4
            other = jnp.where(owner % 2 == core, 0, 1)
            across = jnp.where(which == 0, dz, dy)
            along = jnp.where(which == 0, dy, dz)
            stage = jnp.where(across == 0, 0, jnp.where(across == 2, 2, 1))
            index = jnp.where(along == 0, 0, jnp.where(along == 3, 1, along + 1))
            set_at = other * 2 + which
            near = 2 * set_at + jnp.where(across == 3, 0, 1)
            position = index + 4 * jnp.where(stage == 1, near, set_at)
            base = jnp.where(stage == 0, int(starts[0]), jnp.where(stage == 1, int(starts[1]), int(starts[2])))
            found.append((slot, stage, base + position))
        following = []
        begin = jnp.int32(0)
        for stage in range(STAGES):
            table[SEGMENTS + g * (STAGES + 1) + stage] = begin
            following.append(begin)
            begin = begin + sum(jnp.where(f[1] == stage, 1, 0) for f in found)
        table[SEGMENTS + g * (STAGES + 1) + STAGES] = begin
        for k, (slot, stage, position) in enumerate(found):
            place = jnp.where(stage == 0, following[0], jnp.where(stage == 1, following[1], following[2]))
            following = [f + jnp.where(stage == n, 1, 0) for n, f in enumerate(following)]
            table[SLOTS + g * listed + place] = slot
            table[DEST + position] = g * listed + place
            listing[place] = k
        for s in range(g * SHARE, (g + 1) * SHARE):
            count = counts[s]
            table[COUNTS + s] = count
            for stage in range(STAGES):
                table[LIVES + s * STAGES + stage] = sum(
                    jnp.where((f[1] == stage) & (k < count), 1, 0) for k, f in enumerate(found)
                )
            turn = jnp.int32(0)
            for place in range(listed):
                live = jnp.where(listing[place] < count, 1, 0)
                table[ORDER + s * listed + turn] = place
                table[ALIVE + s * listed + place] = live
                turn = turn + live
    for copy in copies:
        copy.wait()


def tables(pair_list, counts, owner_map, source_vectors, target_blocks):
    listed = pair_list.shape[1]
    me = jnp.reshape(lax.axis_index("row"), (1,)).astype(jnp.int32)
    smem = pl.BlockSpec(memory_space=pltpu.SMEM)
    return pl.pallas_call(
        functools.partial(tables_kernel, target_blocks),
        in_specs=[smem] * 4 + [pl.BlockSpec(memory_space=pltpu.HBM)],
        out_specs=[smem, pl.BlockSpec(memory_space=pltpu.VMEM)],
        out_shape=[
            jax.ShapeDtypeStruct((TABLE,), jnp.int32),
            pltpu.VMEM(source_vectors.shape, source_vectors.dtype),
        ],
        scratch_shapes=[pltpu.SMEM((listed,), jnp.int32), pltpu.SemaphoreType.DMA(source_vectors.shape[:1])],
        compiler_params=pltpu.CompilerParams(vmem_limit_bytes=4 * MIB),
        name="tables",
    )(me, pair_list, counts, owner_map, source_vectors)


def shards(source_vectors, target_vectors, pair_list, counts, owner_map):
    target_blocks, quarter, _ = target_vectors.shape
    listed = pair_list.shape[1]
    targets = owner_map.shape[0]
    source_vectors = pltpu.with_memory_space_constraint(source_vectors, pltpu.HBM)
    table, loaded = tables(pair_list, counts, owner_map, source_vectors, target_blocks)

    def stage(number, pieces, earlier):
        pieces = pieces + [send(piece, 0, 0, 1) for piece in pieces]
        pieces = [pltpu.with_memory_space_constraint(piece, pltpu.HBM) for piece in pieces]
        return score_stage(number, listed, table, loaded, pieces, earlier)

    along_y, along_z = target_vectors[:1], target_vectors[1:]
    arrived = ring_sends(along_y, 0, 1) + ring_sends(along_z, 1, 0)
    *arrived, table, loaded = tie(*arrived, table, loaded)
    loaded = pltpu.with_memory_space_constraint(loaded, pltpu.VMEM)
    first = [jnp.concatenate([along_y] + arrived[:3], axis=0), jnp.concatenate([along_z] + arrived[3:], axis=0)]
    second = [
        send(first[0], 1, 0, 0),
        send(first[0], -1, 0, 0),
        send(first[1], 0, 1, 0),
        send(first[1], 0, -1, 0),
    ]
    done = stage(0, first, [])
    *second, peaks = tie(*second, done[1])
    third = [
        send(second[0][:2], 1, 0, 0),
        send(second[1][2:], -1, 0, 0),
        send(second[2][:2], 0, 1, 0),
        send(second[3][2:], 0, -1, 0),
    ]
    done = stage(1, second, [done[0], peaks, done[2]])
    *third, peaks = tie(*third, done[1])
    matrix, peaks, _, high, total = stage(2, third, [done[0], peaks, done[2]])
    matrix = pltpu.with_memory_space_constraint(matrix, pltpu.VMEM)

    both = from_columns(jnp.stack([high, total]))
    level = jnp.maximum(functools.reduce(jnp.maximum, [b[0] for b in both]), 0.0)
    parts = [b[1] * jnp.exp2(b[0] - level) for b in both]

    for sweep_index in range(SWEEPS):
        final = sweep_index == SWEEPS - 1
        sums = column_pass(final, table, targets, level, parts, matrix, peaks)
        if final:
            break
        sums = sum_over_rows(sums[0])
        parts = from_columns(row_pass(table, level, sums, matrix, peaks))
    sums, source_dual = sums
    row_count = targets // target_blocks
    back = lax.all_to_all(
        sums.reshape(row_count, target_blocks, quarter), "row", split_axis=0, concat_axis=0, tiled=True
    )
    target_dual = -EPSILON * jnp.log(1.0 + jnp.sum(back, axis=0))
    return source_dual, target_dual


def solution(mesh):
    return jax.shard_map(
        shards,
        mesh=mesh,
        in_specs=(P("row", None, None), P("row", "col", None), P("row", None), P("row"), P()),
        out_specs=(P("row", None), P("row", "col")),
        check_vma=False,
    )
```
